32 devices in a mesh: wide: 16 (over z, x, core), narrow: 2 (over y).
Axes of the slice: x: 2, y: 2, z: 4, core: 2. Of those that a mesh axis runs over, the one named last changes fastest.
Arguments:
- tokens: bfloat16 [32, 6144], P('wide', 'narrow'), may hold values from -11 to 11
- norm_gain: bfloat16 [6144], P('narrow'), may hold values from 0.099609375 to 1.8984375
- routes: int32 [4, 32, 2], replicated, may hold values from 0 to 3, all different within a row; in each aligned block of 32 rows (0 to 31, 32 to 63, ..., all dimensions but the last counted through in order) at most 24 rows name the same one
- route_weights: float32 [4, 32, 2], replicated, may hold values from 0.2 to 1.5
- w_gate: bfloat16 [4, 6144, 16384], P(None, 'narrow', 'wide'), may hold values from -0.078125 to 0.078125
- w_up: bfloat16 [4, 6144, 16384], P(None, 'narrow', 'wide'), may hold values from -0.078125 to 0.078125
- w_down: bfloat16 [4, 16384, 6144], P(None, 'wide', 'narrow'), may hold values from -0.046875 to 0.046875
Outputs:
- beams_out: bfloat16 [32, 6144], P('wide', 'narrow')
The draws below stay inside these ranges and needn't reach their ends.
Inputs may be any that keep to these rules, and one draw needn't show every extreme that they name: `routes`: within one decode step no expert is named by more than 24 rows, and the experts of one row differ.
All inputs are finite; a program needn't handle non-finite values.
Results may differ from the reference program's by a relative error of at most 0.028.
Values may be sent and summed in bfloat16 or wider, within the bound.
No kernel may reach another device: no remote copies, remote signals or barrier semaphores. Data moves between devices by JAX's collectives and lax.ppermute only.
A program may use at most 128 MiB of HBM per device.

```python
import math
import jax
import jax.numpy as jnp
import numpy as np
from jax import lax

D = 6144
FF = 16384
EXPERTS = 4
TOP = 2
STEPS = 4
ROWS = 32
CAP = 24
N_NARROW = 2


def draw_tokens(key, part):
    column = jnp.arange(D, dtype=jnp.float32) / (D - 1)
    noise = jnp.clip(jax.random.normal(key, (ROWS, D), jnp.float32), -6.0, 6.0)
    values = noise * jnp.sqrt(1.0 + 2.0 * column)[None, :]
    return values.astype(jnp.bfloat16)


def block_levels(rng, shape, pieces, least, high):
    loudness, own = 1.0, jax.random.fold_in(rng, 6)
    for position, blocks in pieces:
        heights = jnp.exp(jax.random.uniform(jax.random.fold_in(own, position), (blocks,), jnp.float32, least / len(pieces), high / len(pieces)))
        loudness = loudness * jnp.repeat(heights, shape[position] // blocks).reshape([-1 if axis == position else 1 for axis in range(len(shape))])
    return loudness


def deal_out(rng, own, number, rows, number_of, top, bound, skew):
    order = jax.random.permutation(rng, number_of)
    crowded, usual = shares(number_of, rows * top, bound, skew, True), shares(number_of, rows * top, bound, skew, False)
    places = jnp.arange(number_of)

    def named(lengths, rotation):
        used = int((lengths > 0).sum())
        fixed = max(1, used // 4)
        moved = fixed + (places - fixed + rotation * (used - fixed)) % max(1, number_of - fixed)
        return jnp.zeros((number_of,), jnp.int32).at[order[jnp.where(places < fixed, places, moved)]].set(jnp.asarray(lengths, jnp.int32))

    lengths = jnp.where(number % 4 == 0, named(crowded, number // 4), named(usual, number - number // 4 - 1))
    mixed = jax.random.permutation(jax.random.fold_in(own, 3), number_of)
    donor, receiver = mixed[0:number_of // 2 * 2:2], mixed[1:number_of // 2 * 2:2]
    room = jnp.minimum(lengths[donor] - 1, bound - lengths[receiver]) // 2
    room = jnp.where((donor == order[0]) | (receiver == order[0]) | (lengths[receiver] == 0), 0, jnp.maximum(room, 0))
    moved = jax.random.randint(jax.random.fold_in(own, 4), (number_of // 2,), 0, 1 << 20) % (room + 1)
    lengths = lengths.at[donor].add(-moved).at[receiver].add(moved)
    members = jnp.searchsorted(jnp.cumsum(lengths), jnp.arange(rows * top), side="right").astype(jnp.int32)
    listing = members.reshape(top, rows).T
    listing = listing[jax.random.permutation(jax.random.fold_in(own, 1), rows)]
    rotation = jax.random.randint(jax.random.fold_in(own, 2), (rows, 1), 0, top)
    return jnp.take_along_axis(listing, (jnp.arange(top)[None, :] + rotation) % top, axis=1)


def shares(count, total, reach, lean, full):
    weights = [(1 << 20) // math.isqrt(grade ** lean) + 1 for grade in range(1, count + 1)]
    largest = reach if full else min(reach, max(-(-total // count), total * weights[0] // sum(weights)))
    least = 1 if total - largest >= count - 1 else 0
    holding, rest = [largest] + [least] * (count - 1), total - largest - least * (count - 1)
    while rest > 0:
        candidates = [i for i in range(1, count) if holding[i] < largest] or [i for i in range(1, count) if holding[i] < reach]
        mass, remaining = sum([weights[i] for i in candidates]), rest
        for i in candidates:
            more = min(reach - holding[i], max(1, remaining * weights[i] // mass), rest)
            holding[i] = holding[i] + more
            rest = rest - more
    return np.array(holding)


def scatter_about(rng, dims, deviation, most, shards=(), kind=jnp.bfloat16):
    entries = deviation * jax.random.normal(rng, dims, jnp.float32)
    if shards:
        entries = entries * block_levels(rng, dims, shards, -0.22, 0.18)
    return jnp.clip(entries, -most, most).astype(kind)


def setup_inputs(seed: int = 0) -> dict:
    arg_keys = jax.random.split(jax.random.key(seed), 8)
    tokens = draw_tokens(jax.random.fold_in(arg_keys[7], 71), 0)
    norm_gain = jnp.clip(1.0 + 0.18 * jax.random.normal(arg_keys[1], (D,), jnp.float32), 0.099609375, 1.8984375).astype(jnp.bfloat16)
    routes_keys = jax.random.split(jax.random.fold_in(arg_keys[2], 1), STEPS * ROWS // ROWS)
    routes_turns = jax.random.permutation(jax.random.fold_in(arg_keys[2], 3), STEPS * ROWS // ROWS)
    routes = jax.vmap(lambda own, number: deal_out(jax.random.fold_in(arg_keys[2], 2), own, number, ROWS, EXPERTS, TOP, CAP, 1))(routes_keys, routes_turns).reshape((STEPS, ROWS, TOP))
    route_weights = jnp.clip(jnp.exp(jax.random.uniform(arg_keys[3], (STEPS, ROWS, TOP), jnp.float32, math.log(0.2), math.log(1.5))), 0.2, 1.5)
    w_gate = scatter_about(arg_keys[4], (EXPERTS, D, FF), D ** -0.5, 0.078125, ((1, 2), (2, 16)))
    w_up = scatter_about(arg_keys[5], (EXPERTS, D, FF), D ** -0.5, 0.078125, ((1, 2), (2, 16)))
    w_down = scatter_about(arg_keys[6], (EXPERTS, FF, D), FF ** -0.5, 0.046875, ((1, 16), (2, 2)))
    return dict(tokens=tokens, norm_gain=norm_gain, routes=routes, route_weights=route_weights, w_gate=w_gate, w_up=w_up, w_down=w_down)


epsilon = 1e-05

def slot_tables(route_step, experts, capacity):
    count_all = route_step.shape[0] * route_step.shape[1]
    flat_route = route_step.reshape(count_all).astype(jnp.int32)
    onehot = (flat_route[:, None] == jnp.arange(experts, dtype=jnp.int32)[None, :]).astype(jnp.int32)
    before = (jnp.cumsum(onehot, axis=0) - onehot).astype(jnp.int32)
    within = lax.optimization_barrier(jnp.sum(before * onehot, axis=1)).astype(jnp.int32)
    slot_of = (flat_route * capacity + within).astype(jnp.int32)
    source = (jnp.arange(count_all, dtype=jnp.int32) // route_step.shape[1]).astype(jnp.int32)
    slot_row = jnp.zeros((experts * capacity,), jnp.int32).at[slot_of].set(source)
    slot_live = jnp.zeros((experts * capacity,), jnp.int32).at[slot_of].set(1)
    return (slot_of.reshape(route_step.shape), slot_row, slot_live)

def blocked_product(rows_in, weight):
    parts = rows_in.astype(jnp.float32).reshape(CAP, N_NARROW, D // N_NARROW)
    blocks = weight.astype(jnp.float32).reshape(N_NARROW, D // N_NARROW, FF)
    partial_sums = jnp.einsum('cnd,ndf->ncf', parts, blocks)
    rounded = lax.optimization_barrier(partial_sums.astype(jnp.bfloat16)).astype(jnp.float32)
    return lax.optimization_barrier(jnp.sum(rounded, axis=0))

def run_expert(operands):
    rows_in, gate_w, up_w, down_w = operands
    gate_sum = blocked_product(rows_in, gate_w)
    up_sum = blocked_product(rows_in, up_w)
    hidden = (jax.nn.silu(gate_sum) * up_sum).astype(jnp.bfloat16)
    return jnp.dot(hidden, down_w, preferred_element_type=jnp.float32)

def reference(tokens, norm_gain, routes, route_weights, w_gate, w_up, w_down):
    gain_row = norm_gain.astype(jnp.float32)
    current = tokens
    for turn_index in range(STEPS):
        values = current.astype(jnp.float32)
        mean_square = lax.optimization_barrier(jnp.mean(values * values, axis=1, keepdims=True))
        normed = (values * lax.rsqrt(mean_square + epsilon) * gain_row[None, :]).astype(jnp.bfloat16)
        slot_of, slot_row, slot_live = slot_tables(routes[turn_index], EXPERTS, CAP)
        picked = jnp.where(slot_live[:, None] > 0, normed[slot_row], jnp.zeros((), jnp.bfloat16))
        picked = picked.reshape(EXPERTS, CAP, D)
        expert_out = lax.map(run_expert, (picked, w_gate, w_up, w_down)).reshape(EXPERTS * CAP, D)
        weights = route_weights[turn_index]
        combined = weights[:, 0:1] * expert_out[slot_of[:, 0]]
        for route_k in range(1, TOP):
            combined = combined + weights[:, route_k:route_k + 1] * expert_out[slot_of[:, route_k]]
        current = (current.astype(jnp.float32) + combined).astype(jnp.bfloat16)
    return current
```

```python
import functools

import jax
import jax.numpy as jnp
from jax import lax
from jax.experimental import pallas as pl
from jax.experimental.pallas import tpu as pltpu
from jax.sharding import PartitionSpec as P

epsilon = 1e-05
MIB = 1 << 20
VMEM = pl.BlockSpec(memory_space=pltpu.VMEM)
SMEM = pl.BlockSpec(memory_space=pltpu.SMEM)
HBM = pl.BlockSpec(memory_space=pltpu.HBM)
GROUP = 4
SLOTS = 4
LIMIT = 4 * MIB
FIRST_LIMIT = 11 * MIB


def in_vmem(array):
    return pltpu.with_memory_space_constraint(array, pltpu.VMEM)


def in_hbm(array):
    return pltpu.with_memory_space_constraint(array, pltpu.HBM)


def with_weights(kernel, inputs, kept, specs, shapes, scratch, name, limit=None, **cost):
    count = len(inputs)

    def run(*refs):
        kernel(refs[count : count + len(kept)], *refs[:count], *refs[count + len(kept) :])

    more = {"cost_estimate": pl.CostEstimate(transcendentals=0, **cost)} if cost else {}
    return pl.pallas_call(
        run,
        in_specs=specs + [VMEM] * len(kept),
        out_specs=[VMEM] * len(shapes),
        out_shape=shapes,
        scratch_shapes=scratch,
        name=name,
        compiler_params=pltpu.CompilerParams(vmem_limit_bytes=limit or LIMIT),
        **more,
    )(*inputs, *[in_vmem(weight) for weight in kept])


def prepare_kernel(place, gain, named, weight, *outs):
    place_out, gain_out, marks = outs[0], outs[1], outs[2:]
    for i in range(3):
        place_out[i] = place[i]
    gain_out[...] = gain[...].astype(jnp.float32)
    for step, mark in enumerate(marks):
        column = lax.broadcasted_iota(jnp.int32, mark.shape, 1)
        experts = mark.shape[1] // 2
        expert = jnp.where(column < experts, column, column - experts)
        value = jnp.where(column < experts, weight[step], 1.0)
        mark[...] = jnp.where(named[step] == expert, value, 0.0)


def prepare(place, gain, routes, route_weights, experts):
    steps, rows, top = routes.shape
    named = jnp.swapaxes(routes, 1, 2).reshape(steps, top * rows, 1)
    weight = jnp.swapaxes(route_weights, 1, 2).reshape(steps, top * rows, 1)
    place, gain, *marks = pl.pallas_call(
        prepare_kernel,
        in_specs=[SMEM] + [VMEM] * 3,
        out_specs=[SMEM] + [VMEM] * (1 + steps),
        out_shape=[jax.ShapeDtypeStruct((3,), jnp.int32), jax.ShapeDtypeStruct((1, gain.shape[0]), jnp.float32)]
        + [jax.ShapeDtypeStruct((top * rows, 2 * experts), jnp.float32)] * steps,
        name="prepare",
        compiler_params=pltpu.CompilerParams(vmem_limit_bytes=4 * MIB),
    )(place, gain.reshape(1, -1), named, weight)
    return place, gain, marks


def pack_kernel(a, b, c, d, out, rows):
    for k, ref in enumerate((a, b, c, d)):
        rows[2 * k : 2 * k + 2, :] = ref[...].astype(jnp.float32)
    out[...] = rows[...].astype(out.dtype)


def pack(parts):
    depth = parts[0].shape[1]
    return pl.pallas_call(
        pack_kernel,
        in_specs=[VMEM] * 4,
        out_specs=VMEM,
        out_shape=jax.ShapeDtypeStruct((8, depth), jnp.bfloat16),
        scratch_shapes=[pltpu.VMEM((8, depth), jnp.float32)],
        name="pack",
        compiler_params=pltpu.CompilerParams(vmem_limit_bytes=MIB),
    )(*parts)


def rows_of(count, all_rows, wanted):
    row = lax.broadcasted_iota(jnp.int32, (count, all_rows), 0)
    column = lax.broadcasted_iota(jnp.int32, (count, all_rows), 1)
    return jnp.where(wanted(row) == column, 1.0, 0.0).astype(jnp.bfloat16)


def pick(matrix, rows):
    return jnp.dot(matrix, rows.astype(jnp.bfloat16), preferred_element_type=jnp.float32)


def split_kernel(_, place, a, b, c, d, *refs):
    outs, rows = refs[:-1], refs[-1]
    mine, line = place[0], place[1]
    for o, ref in enumerate((a, b, c, d)):
        rows[8 * o : 8 * o + 8, :] = ref[...].astype(jnp.float32)

    def source(row):
        return 8 * (((row >> 1) & 3) ^ mine) + 2 * ((row >> 3) ^ line) + (row & 1)

    count = rows.shape[0]
    rows[...] = pick(rows_of(count, count, source), rows[...])
    piece = outs[0].shape[1]
    for o in range(GROUP):
        at = pl.ds(pl.multiple_of((mine ^ o) * piece, 128), piece)
        outs[o][...] = rows[:, at].astype(jnp.bfloat16)


def split(place, parts, kept):
    depth = parts[0].shape[1]
    rows = GROUP * parts[0].shape[0]
    return with_weights(
        split_kernel,
        [place, *parts],
        [],
        [SMEM] + [VMEM] * 4,
        [jax.ShapeDtypeStruct((rows, depth // GROUP), jnp.bfloat16)] * GROUP,
        [pltpu.VMEM((rows, depth), jnp.float32)],
        "split",
    )


def sum_kernel(_, *refs):
    total = refs[0][...].astype(jnp.float32)
    for ref in refs[1:-1]:
        total = total + ref[...].astype(jnp.float32)
    refs[-1][...] = total.astype(refs[-1].dtype)


def add_up(parts, kept):
    shapes = [jax.ShapeDtypeStruct(parts[0].shape, jnp.bfloat16)]
    return with_weights(sum_kernel, parts, [], [VMEM] * len(parts), shapes, [], "add_up")[0]


def finish_kernel(_, place, s0, s1, s2, s3, x0, x1, x2, x3, out, rows, total):
    mine, line, index = place[0], place[1], place[2]
    for k, ref in enumerate((s0, s1, s2, s3)):
        total[8 * k : 8 * k + 8, :] = ref[...].astype(jnp.float32)
    piece = x0.shape[1]
    for o, ref in enumerate((x0, x1, x2, x3)):
        at = pl.ds(pl.multiple_of((mine ^ o) * piece, 128), piece)
        rows[:, at] = ref[...].astype(jnp.float32)
    count = rows.shape[0]
    result = pick(rows_of(16, count, lambda row: 2 * index + row), rows[...])
    for k in range(GROUP):
        result = result + pick(rows_of(16, count, lambda row: 8 * k + 2 * line + row), total[...])
    out[...] = result[0:2, :].astype(out.dtype)


def finish(place, sums, pieces, kept):
    depth = sums[0].shape[1]
    rows = pieces[0].shape[0]
    return with_weights(
        finish_kernel,
        [place, *sums, *pieces],
        [],
        [SMEM] + [VMEM] * 8,
        [jax.ShapeDtypeStruct((2, depth), jnp.bfloat16)],
        [pltpu.VMEM((rows, depth), jnp.float32)] * 2,
        "finish",
    )[0]


def load_kernel(first, place, w_gate, w_up, w_down, tail, down, sem):
    del place
    experts, depth, hidden = w_gate.shape
    last = hidden - first
    copies = []

    def put(source, target):
        copies.append(pltpu.make_async_copy(source, target, sem.at[len(copies)]))

    for e in range(experts):
        for m, weight in enumerate((w_gate, w_up)):
            put(weight.at[e, :, pl.ds(first, last)], tail.at[:, pl.ds((2 * e + m) * last, last)])
        put(w_down.at[e], down.at[e])
    for copy in copies:
        copy.start()
    for copy in copies:
        copy.wait()


def load_weights(place, w_gate, w_up, w_down, first):
    experts, depth, hidden = w_gate.shape
    last = hidden - first
    kind = w_gate.dtype
    return pl.pallas_call(
        functools.partial(load_kernel, first),
        in_specs=[SMEM] + [HBM] * 3,
        out_specs=[VMEM] * 2,
        out_shape=[pltpu.VMEM((depth, 2 * experts * last), kind), pltpu.VMEM(w_down.shape, kind)],
        scratch_shapes=[pltpu.SemaphoreType.DMA((3 * experts,))],
        name="load_weights",
        cost_estimate=pl.CostEstimate(flops=0, bytes_accessed=36 * MIB, transcendentals=0),
        compiler_params=pltpu.CompilerParams(vmem_limit_bytes=LIMIT),
    )(place, in_hbm(w_gate), in_hbm(w_up), in_hbm(w_down))


def first_kernel(
    first, kept, place, x0, x1, x2, x3, gain, marks, w_gate, w_up, chosen, scaled, squares, ring, total, sem
):
    experts, depth, _ = w_gate.shape
    rows, piece = x0.shape
    block = depth // GROUP
    streamed = [(e, q) for e in range(experts) for q in range(GROUP)]

    def copies(i):
        e, q = streamed[i]
        slot = i % SLOTS
        return [
            pltpu.make_async_copy(
                weight.at[e, pl.ds(q * block, block), pl.ds(0, first)],
                ring.at[slot, :, pl.ds(m * first, first)],
                sem.at[slot, m],
            )
            for m, weight in enumerate((w_gate, w_up))
        ]

    for i in range(min(SLOTS, len(streamed))):
        for copy in copies(i):
            copy.start()

    mine = place[0]
    square = jnp.zeros((rows, 1), jnp.float32)
    for o, ref in enumerate((x0, x1, x2, x3)):
        at = pl.ds(pl.multiple_of((mine ^ o) * piece, 128), piece)
        values = ref[...].astype(jnp.float32)
        square = square + jnp.sum(values * values, axis=1, keepdims=True)
        scaled[:, at] = (values * gain[:, at]).astype(jnp.bfloat16)
    coarse = square.astype(jnp.bfloat16)
    fine = (square - coarse.astype(jnp.float32)).astype(jnp.bfloat16)
    squares[0:rows, :] = jnp.broadcast_to(coarse, (rows, 128))
    squares[rows : 2 * rows, :] = jnp.broadcast_to(fine, (rows, 128))

    started = set()

    def add(e, q, weight):
        product = jnp.dot(
            scaled[:, q * block : (q + 1) * block], weight, preferred_element_type=jnp.float32
        )
        if e in started:
            total[e] += product
        else:
            total[e] = product
            started.add(e)

    for i, (e, q) in enumerate(streamed):
        for copy in copies(i):
            copy.wait()
        add(e, q, ring[i % SLOTS])
        if i + SLOTS < len(streamed):
            for copy in copies(i + SLOTS):
                copy.start()
    for k in range(2):
        picked = jnp.zeros((rows, 2 * first), jnp.float32)
        for e in range(experts):
            mark = marks[k * rows : (k + 1) * rows, experts + e : experts + e + 1]
            picked = jnp.where(mark > 0, total[e], picked)
        chosen[k * rows : (k + 1) * rows, :] = picked.astype(jnp.bfloat16)


def first_columns(place, pieces, gain, marks, kept, w_gate, w_up, first):
    experts, depth, _ = w_gate.shape
    rows = pieces[0].shape[0]
    count = experts * 2 * depth * first
    return with_weights(
        functools.partial(first_kernel, first),
        [place, *pieces, gain, marks, in_hbm(w_gate), in_hbm(w_up)],
        [],
        [SMEM] + [VMEM] * 6 + [HBM] * 2,
        [
            jax.ShapeDtypeStruct((2 * rows, 2 * first), jnp.bfloat16),
            jax.ShapeDtypeStruct((rows, depth), jnp.bfloat16),
            jax.ShapeDtypeStruct((2 * rows, 128), jnp.bfloat16),
        ],
        [
            pltpu.VMEM((SLOTS, depth // GROUP, 2 * first), jnp.bfloat16),
            pltpu.VMEM((experts, rows, 2 * first), jnp.float32),
            pltpu.SemaphoreType.DMA((SLOTS, 2)),
        ],
        "gate_up_first",
        limit=FIRST_LIMIT,
        flops=2 * rows * count,
        bytes_accessed=2 * count,
    )


def last_kernel(last, kept, scaled, squares, marks, chosen):
    tail = kept[0]
    rows = scaled.shape[0]
    experts = tail.shape[1] // (2 * last)
    product = jnp.dot(scaled[...], tail[...], preferred_element_type=jnp.float32)
    for k in range(2):
        picked = jnp.zeros((rows, 2 * last), jnp.float32)
        for e in range(experts):
            mark = marks[k * rows : (k + 1) * rows, experts + e : experts + e + 1]
            picked = jnp.where(mark > 0, product[:, e * 2 * last : (e + 1) * 2 * last], picked)
        chosen[k * rows : (k + 1) * rows, 0 : 2 * last] = picked.astype(jnp.bfloat16)
    chosen[:, 2 * last : 2 * last + 128] = squares[...]


def last_columns(scaled, squares, marks, kept, last):
    rows, size = scaled.shape[0], kept[0].size
    return with_weights(
        functools.partial(last_kernel, last),
        [scaled, squares, marks],
        kept[:1],
        [VMEM] * 3,
        [jax.ShapeDtypeStruct((2 * rows, 2 * last + 128), jnp.bfloat16)],
        [],
        "gate_up_last",
        flops=2 * rows * size,
        bytes_accessed=2 * size,
    )[0]


def down_kernel(width, whole, kept, place, a1, b1, a2, b2, marks, *refs):
    down = kept[0]
    experts, hidden, depth = down.shape
    rows = a1.shape[0] // 2
    first = a1.shape[1] // 2
    last = hidden - first
    outs, total = refs[:-1], refs[-1]

    def both(a, b, start, size):
        return a[:, start : start + size].astype(jnp.float32) + b[:, start : start + size].astype(jnp.float32)

    square = both(a2, b2, 2 * last, 128)
    square = square[0:rows, 0:1] + square[rows : 2 * rows, 0:1]
    scale = lax.rsqrt(square / width + epsilon)
    scale = jnp.concatenate([scale, scale], axis=0)
    parts = []
    for a, b, size in ((a1, b1, first), (a2, b2, last)):
        gate = both(a, b, 0, size) * scale
        up = both(a, b, size, size) * scale
        parts.append(gate / (1.0 + jnp.exp(-gate)) * up)
    value = jnp.concatenate(parts, axis=1)
    mixed = []
    for e in range(experts):
        mixed.append(
            (
                value[0:rows] * marks[0:rows, e : e + 1] + value[rows : 2 * rows] * marks[rows : 2 * rows, e : e + 1]
            ).astype(jnp.bfloat16)
        )
    piece = depth // GROUP
    for n in range(GROUP):
        at = slice(n * piece, (n + 1) * piece)
        acc = jnp.dot(mixed[0], down[0, :, at], preferred_element_type=jnp.float32)
        for e in range(1, experts):
            acc = acc + jnp.dot(mixed[e], down[e, :, at], preferred_element_type=jnp.float32)
        total[:, at] = acc
    mine = place[0]
    for o in range(GROUP):
        if whole:
            matrix = rows_of(16, rows, lambda row: 8 * (row >> 1) + 2 * (mine ^ o) + (row & 1))
            outs[o][...] = pick(matrix, total[...])[0:8, :].astype(outs[o].dtype)
        else:
            at = pl.ds(pl.multiple_of((mine ^ o) * piece, 128), piece)
            outs[o][...] = total[:, at].astype(outs[o].dtype)


def down_product(place, a1, b1, a2, b2, marks, kept, width, whole):
    depth, size = kept[1].shape[2], kept[1].size
    rows = a1.shape[0] // 2
    piece = depth // GROUP
    shape = (2 * GROUP, depth) if whole else (rows, piece)
    shapes = [jax.ShapeDtypeStruct(shape, jnp.float32)]
    shapes += [jax.ShapeDtypeStruct(shape, jnp.bfloat16)] * (GROUP - 1)
    return with_weights(
        functools.partial(down_kernel, width, whole),
        [place, a1, b1, a2, b2, marks],
        kept[1:],
        [SMEM] + [VMEM] * 5,
        shapes,
        [pltpu.VMEM((rows, depth), jnp.float32)],
        "down",
        flops=2 * rows * size,
        bytes_accessed=2 * size,
    )


def swap(value, axis, offset):
    size = lax.axis_size(axis)
    return lax.ppermute(value, axis, [(i, i ^ offset) for i in range(size)])


def body(tokens, norm_gain, routes, route_weights, w_gate, w_up, w_down):
    steps, rows, top = routes.shape
    experts, depth, hidden = w_gate.shape
    width = depth * lax.axis_size("narrow")
    first = 3 * hidden // 4
    last = hidden - first
    index = lax.axis_index("wide").astype(jnp.int32)
    place = jnp.stack([index % GROUP, index // GROUP, index])
    place, gain, marks = prepare(place, norm_gain, routes, route_weights, experts)

    def around(value, scale):
        return [value] + [swap(value, "wide", scale * o) for o in range(1, GROUP)]

    held = pack(around(tokens, GROUP))
    kept = load_weights(place, w_gate, w_up, w_down, first)
    pieces = split(place, around(held, 1), kept)
    for step in range(steps):
        a1, scaled, squares = first_columns(place, pieces, gain, marks[step], kept, w_gate, w_up, first)
        b1 = swap(a1, "narrow", 1)
        a2 = last_columns(scaled, squares, marks[step], kept, last)
        b2 = swap(a2, "narrow", 1)
        final = step == steps - 1
        parts = down_product(place, a1, b1, a2, b2, marks[step], kept, width, final)
        own = add_up([parts[0]] + [swap(parts[o], "wide", o) for o in range(1, GROUP)], kept)
        sums = around(own, GROUP)
        if final:
            return finish(place, sums, pieces, kept)
        pieces = around(add_up([pieces[0]] + sums, kept), 1)


def plain_body(tokens, norm_gain, routes, route_weights, w_gate, w_up, w_down):
    experts = w_gate.shape[0]
    steps, rows, top = routes.shape
    width = tokens.shape[1] * lax.axis_size("narrow")
    gain = norm_gain.astype(jnp.float32)
    named = (routes[..., None] == jnp.arange(experts, dtype=jnp.int32)).astype(jnp.float32)
    current = tokens
    for step in range(steps):
        values = current.astype(jnp.float32)
        squares = lax.psum(jnp.sum(values * values, axis=1), "narrow")
        normed = (values * lax.rsqrt(squares[:, None] / width + epsilon) * gain[None, :]).astype(jnp.bfloat16)
        normed = lax.all_gather(normed, "wide", axis=0, tiled=True)
        gate = jnp.einsum("rd,edf->erf", normed, w_gate, preferred_element_type=jnp.float32)
        up = jnp.einsum("rd,edf->erf", normed, w_up, preferred_element_type=jnp.float32)
        gate = lax.psum(gate.astype(jnp.bfloat16), "narrow").astype(jnp.float32)
        up = lax.psum(up.astype(jnp.bfloat16), "narrow").astype(jnp.float32)
        value = (jax.nn.silu(gate) * up).astype(jnp.bfloat16)
        out = jnp.einsum("erf,efd->erd", value, w_down, preferred_element_type=jnp.float32)
        share = jnp.sum(named[step] * route_weights[step][..., None], axis=1)
        combined = jnp.einsum("re,erd->rd", share, out, precision=lax.Precision.HIGHEST)
        summed = lax.psum_scatter(combined, "wide", scatter_dimension=0, tiled=True)
        current = (current.astype(jnp.float32) + summed).astype(jnp.bfloat16)
    return current


def solution(mesh):
    placed = (
        P("wide", "narrow"),
        P("narrow"),
        P(),
        P(),
        P(None, "narrow", "wide"),
        P(None, "narrow", "wide"),
        P(None, "wide", "narrow"),
    )

    def call(*args):
        tokens, _, routes, _, w_gate, _, _ = args
        wide, narrow = mesh.shape["wide"], mesh.shape["narrow"]
        depth, hidden = w_gate.shape[1] // narrow, w_gate.shape[2] // wide
        routes = args[2]
        fits = narrow == 2 and wide == GROUP * GROUP and routes.shape[2] == 2 and w_gate.shape[0] >= 2
        fits = fits and depth % (GROUP * 128) == 0 and hidden % 512 == 0 and routes.shape[1] == 2 * GROUP * GROUP
        return jax.shard_map(
            body if fits else plain_body, mesh=mesh, in_specs=placed, out_specs=P("wide", "narrow"), check_vma=False
        )(*args)

    return call
```

```python
import functools

import jax
import jax.numpy as jnp
from jax import lax
from jax.experimental import pallas as pl
from jax.experimental.pallas import tpu as pltpu
from jax.sharding import PartitionSpec as P

epsilon = 1e-05
MIB = 1 << 20
VMEM = pl.BlockSpec(memory_space=pltpu.VMEM)
SMEM = pl.BlockSpec(memory_space=pltpu.SMEM)
HBM = pl.BlockSpec(memory_space=pltpu.HBM)
GROUP = 4
SLOTS = 4
KEPT = 2
NOTE = jax.ShapeDtypeStruct((8, 128), jnp.float32)
LIMIT = 2 * MIB
FIRST_LIMIT = 8 * MIB


def in_vmem(array):
    return pltpu.with_memory_space_constraint(array, pltpu.VMEM)


def in_hbm(array):
    return pltpu.with_memory_space_constraint(array, pltpu.HBM)


def with_weights(kernel, inputs, kept, specs, shapes, scratch, name, limit=None, **cost):
    count = len(inputs)

    def run(*refs):
        kernel(refs[count : count + len(kept)], *refs[:count], *refs[count + len(kept) :])

    more = {"cost_estimate": pl.CostEstimate(transcendentals=0, **cost)} if cost else {}
    return pl.pallas_call(
        run,
        in_specs=specs + [VMEM] * len(kept),
        out_specs=[VMEM] * len(shapes),
        out_shape=shapes,
        scratch_shapes=scratch,
        name=name,
        compiler_params=pltpu.CompilerParams(vmem_limit_bytes=limit or LIMIT),
        **more,
    )(*inputs, *[in_vmem(weight) for weight in kept])


def prepare_kernel(place, gain, named, weight, *outs):
    place_out, gain_out, marks = outs[0], outs[1], outs[2:]
    for i in range(3):
        place_out[i] = place[i]
    gain_out[...] = gain[...].astype(jnp.float32)
    for step, mark in enumerate(marks):
        column = lax.broadcasted_iota(jnp.int32, mark.shape, 1)
        experts = mark.shape[1] // 2
        expert = jnp.where(column < experts, column, column - experts)
        value = jnp.where(column < experts, weight[step], 1.0)
        mark[...] = jnp.where(named[step] == expert, value, 0.0)


def prepare(place, gain, routes, route_weights, experts):
    steps, rows, top = routes.shape
    named = jnp.swapaxes(routes, 1, 2).reshape(steps, top * rows, 1)
    weight = jnp.swapaxes(route_weights, 1, 2).reshape(steps, top * rows, 1)
    place, gain, *marks = pl.pallas_call(
        prepare_kernel,
        in_specs=[SMEM] + [VMEM] * 3,
        out_specs=[SMEM] + [VMEM] * (1 + steps),
        out_shape=[jax.ShapeDtypeStruct((3,), jnp.int32), jax.ShapeDtypeStruct((1, gain.shape[0]), jnp.float32)]
        + [jax.ShapeDtypeStruct((top * rows, 2 * experts), jnp.float32)] * steps,
        name="prepare",
        compiler_params=pltpu.CompilerParams(vmem_limit_bytes=4 * MIB),
    )(place, gain.reshape(1, -1), named, weight)
    return place, gain, marks


def pack_kernel(note, a, b, c, d, out, note_out, rows):
    note_out[...] = note[...]
    for k, ref in enumerate((a, b, c, d)):
        rows[2 * k : 2 * k + 2, :] = ref[...].astype(jnp.float32)
    out[...] = rows[...].astype(out.dtype)


def pack(note, parts):
    depth = parts[0].shape[1]
    return pl.pallas_call(
        pack_kernel,
        in_specs=[VMEM] * 5,
        out_specs=[VMEM] * 2,
        out_shape=[jax.ShapeDtypeStruct((8, depth), jnp.bfloat16), NOTE],
        scratch_shapes=[pltpu.VMEM((8, depth), jnp.float32)],
        name="pack",
        compiler_params=pltpu.CompilerParams(vmem_limit_bytes=MIB),
    )(note, *parts)


def rows_of(count, all_rows, wanted):
    row = lax.broadcasted_iota(jnp.int32, (count, all_rows), 0)
    column = lax.broadcasted_iota(jnp.int32, (count, all_rows), 1)
    return jnp.where(wanted(row) == column, 1.0, 0.0).astype(jnp.bfloat16)


def pick(matrix, rows):
    return jnp.dot(matrix, rows.astype(jnp.bfloat16), preferred_element_type=jnp.float32)


def split_kernel(_, place, a, b, c, d, *refs):
    outs, rows = refs[:-1], refs[-1]
    mine, line = place[0], place[1]
    for o, ref in enumerate((a, b, c, d)):
        rows[8 * o : 8 * o + 8, :] = ref[...].astype(jnp.float32)

    def source(row):
        return 8 * (((row >> 1) & 3) ^ mine) + 2 * ((row >> 3) ^ line) + (row & 1)

    count = rows.shape[0]
    rows[...] = pick(rows_of(count, count, source), rows[...])
    piece = outs[0].shape[1]
    for o in range(GROUP):
        at = pl.ds(pl.multiple_of((mine ^ o) * piece, 128), piece)
        outs[o][...] = rows[:, at].astype(jnp.bfloat16)


def split(place, parts):
    depth = parts[0].shape[1]
    rows = GROUP * parts[0].shape[0]
    return with_weights(
        split_kernel,
        [place, *parts],
        [],
        [SMEM] + [VMEM] * 4,
        [jax.ShapeDtypeStruct((rows, depth // GROUP), jnp.bfloat16)] * GROUP,
        [pltpu.VMEM((rows, depth), jnp.float32)],
        "split",
    )


def sum_kernel(_, *refs):
    total = refs[0][...].astype(jnp.float32)
    for ref in refs[1:-1]:
        total = total + ref[...].astype(jnp.float32)
    refs[-1][...] = total.astype(refs[-1].dtype)


def add_up(parts):
    shapes = [jax.ShapeDtypeStruct(parts[0].shape, jnp.bfloat16)]
    return with_weights(sum_kernel, parts, [], [VMEM] * len(parts), shapes, [], "add_up")[0]


def finish_kernel(_, place, s0, s1, s2, s3, x0, x1, x2, x3, out, rows, total):
    mine, line, index = place[0], place[1], place[2]
    for k, ref in enumerate((s0, s1, s2, s3)):
        total[8 * k : 8 * k + 8, :] = ref[...].astype(jnp.float32)
    piece = x0.shape[1]
    for o, ref in enumerate((x0, x1, x2, x3)):
        at = pl.ds(pl.multiple_of((mine ^ o) * piece, 128), piece)
        rows[:, at] = ref[...].astype(jnp.float32)
    count = rows.shape[0]
    result = pick(rows_of(16, count, lambda row: 2 * index + row), rows[...])
    for k in range(GROUP):
        result = result + pick(rows_of(16, count, lambda row: 8 * k + 2 * line + row), total[...])
    out[...] = result[0:2, :].astype(out.dtype)


def finish(place, sums, pieces):
    depth = sums[0].shape[1]
    rows = pieces[0].shape[0]
    return with_weights(
        finish_kernel,
        [place, *sums, *pieces],
        [],
        [SMEM] + [VMEM] * 8,
        [jax.ShapeDtypeStruct((2, depth), jnp.bfloat16)],
        [pltpu.VMEM((rows, depth), jnp.float32)] * 2,
        "finish",
    )[0]


def load_down_kernel(place, w_down, down, note, sem):
    del place
    copies = [pltpu.make_async_copy(w_down.at[e], down.at[e], sem.at[e]) for e in range(w_down.shape[0])]
    for copy in copies:
        copy.start()
    note[...] = jnp.zeros_like(note)
    for copy in copies:
        copy.wait()


def load_down(place, w_down):
    return pl.pallas_call(
        load_down_kernel,
        in_specs=[SMEM, HBM],
        out_specs=[VMEM] * 2,
        out_shape=[pltpu.VMEM(w_down.shape, w_down.dtype), NOTE],
        scratch_shapes=[pltpu.SemaphoreType.DMA((w_down.shape[0],))],
        name="load_down",
        cost_estimate=pl.CostEstimate(flops=0, bytes_accessed=2 * w_down.size, transcendentals=0),
        compiler_params=pltpu.CompilerParams(vmem_limit_bytes=LIMIT),
    )(place, in_hbm(w_down))


def load_heads_kernel(note, w_gate, w_up, *refs):
    del note
    heads, sem = refs[:-1], refs[-1]
    half = w_gate.shape[2] // len(heads)
    copies = []
    for c, head in enumerate(heads):
        for e in range(head.shape[0]):
            for m, weight in enumerate((w_gate, w_up)):
                copies.append(
                    pltpu.make_async_copy(
                        weight.at[e, :, pl.ds(c * half, half)],
                        head.at[e, :, pl.ds(m * half, half)],
                        sem.at[len(copies)],
                    )
                )
    for copy in copies:
        copy.start()
    for copy in copies:
        copy.wait()


def load_heads(note, w_gate, w_up):
    _, depth, hidden = w_gate.shape
    head = pltpu.VMEM((KEPT, depth, hidden), w_gate.dtype)
    return pl.pallas_call(
        load_heads_kernel,
        in_specs=[VMEM] + [HBM] * 2,
        out_specs=[VMEM] * 2,
        out_shape=[head, head],
        scratch_shapes=[pltpu.SemaphoreType.DMA((4 * KEPT,))],
        name="load_heads",
        cost_estimate=pl.CostEstimate(flops=0, bytes_accessed=24 * MIB, transcendentals=0),
        compiler_params=pltpu.CompilerParams(vmem_limit_bytes=LIMIT),
    )(note, in_hbm(w_gate), in_hbm(w_up))


def scale_up(place, pieces, gain, scaled, chosen, start):
    rows, piece = pieces[0].shape
    mine = place[0]
    square = jnp.zeros((rows, 1), jnp.float32)
    for o, ref in enumerate(pieces):
        at = pl.ds(pl.multiple_of((mine ^ o) * piece, 128), piece)
        values = ref[...].astype(jnp.float32)
        square = square + jnp.sum(values * values, axis=1, keepdims=True)
        scaled[:, at] = (values * gain[:, at]).astype(jnp.bfloat16)
    coarse = square.astype(jnp.bfloat16)
    fine = (square - coarse.astype(jnp.float32)).astype(jnp.bfloat16)
    chosen[0:rows, start : start + 128] = jnp.broadcast_to(coarse, (rows, 128))
    chosen[rows : 2 * rows, start : start + 128] = jnp.broadcast_to(fine, (rows, 128))


def half_product(start, kept, scaled, marks, w_gate, w_up, chosen, ring, total, sem, before=None):
    (head,) = kept
    experts, depth, _ = w_gate.shape
    half = ring.shape[2] // 2
    rows = total.shape[1]
    block = ring.shape[1]
    streamed = [(e, q) for e in range(head.shape[0], experts) for q in range(depth // block)]
    resident = [(e, q) for e in range(head.shape[0]) for q in range(depth // block)]

    def copies(i):
        e, q = streamed[i]
        slot = i % SLOTS
        return [
            pltpu.make_async_copy(
                weight.at[e, pl.ds(q * block, block), pl.ds(start, half)],
                ring.at[slot, :, pl.ds(m * half, half)],
                sem.at[slot, m],
            )
            for m, weight in enumerate((w_gate, w_up))
        ]

    for i in range(min(SLOTS, len(streamed))):
        for copy in copies(i):
            copy.start()
    if before is not None:
        before()

    def add(e, q, weight):
        product = jnp.dot(
            scaled[:, q * block : (q + 1) * block], weight, preferred_element_type=jnp.float32
        )
        if q:
            total[e] += product
        else:
            total[e] = product

    ahead = max(len(resident) - len(streamed) // 2 + 1, 0)
    for i in range(ahead):
        e, q = resident[i]
        add(e, q, head[e, q * block : (q + 1) * block, :])
    left = resident[ahead:]
    for i in range(len(streamed)):
        for copy in copies(i):
            copy.wait()
        add(*streamed[i], ring[i % SLOTS])
        if i + SLOTS < len(streamed):
            for copy in copies(i + SLOTS):
                copy.start()
        if left and (i % 2 == 1 or i + 1 == len(streamed)):
            for e, q in left if i + 1 == len(streamed) else left[:1]:
                add(e, q, head[e, q * block : (q + 1) * block, :])
            left = left[1:]
    for k in range(2):
        picked = jnp.zeros((rows, 2 * half), jnp.float32)
        for e in range(experts):
            mark = marks[k * rows : (k + 1) * rows, experts + e : experts + e + 1]
            picked = jnp.where(mark > 0, total[e], picked)
        chosen[k * rows : (k + 1) * rows, 0 : 2 * half] = picked.astype(jnp.bfloat16)


def first_kernel(kept, place, x0, x1, x2, x3, gain, marks, w_gate, w_up, chosen, scaled, ring, total, sem):
    half_product(
        0, kept, scaled, marks, w_gate, w_up, chosen, ring, total, sem,
        before=lambda: scale_up(place, (x0, x1, x2, x3), gain, scaled, chosen, ring.shape[2]),
    )


def last_kernel(kept, scaled, marks, w_gate, w_up, chosen, ring, total, sem):
    half_product(ring.shape[2] // 2, kept, scaled, marks, w_gate, w_up, chosen, ring, total, sem)


def half_columns(kernel, inputs, specs, kept, w_gate, w_up, outs, name):
    experts, depth, hidden = w_gate.shape
    rows = outs[0].shape[0] // 2
    count = experts * depth * hidden
    return with_weights(
        kernel,
        [*inputs, in_hbm(w_gate), in_hbm(w_up)],
        [kept],
        specs + [HBM] * 2,
        outs,
        [
            pltpu.VMEM((SLOTS, depth // GROUP, hidden), jnp.bfloat16),
            pltpu.VMEM((experts, rows, hidden), jnp.float32),
            pltpu.SemaphoreType.DMA((SLOTS, 2)),
        ],
        name,
        limit=FIRST_LIMIT,
        flops=2 * rows * count,
        bytes_accessed=2 * count,
    )


def first_columns(place, pieces, gain, marks, kept, w_gate, w_up):
    _, depth, hidden = w_gate.shape
    rows = pieces[0].shape[0]
    outs = [
        jax.ShapeDtypeStruct((2 * rows, hidden + 128), jnp.bfloat16),
        jax.ShapeDtypeStruct((rows, depth), jnp.bfloat16),
    ]
    return half_columns(
        first_kernel, [place, *pieces, gain, marks], [SMEM] + [VMEM] * 6, kept, w_gate, w_up, outs, "gate_up_first"
    )


def last_columns(scaled, marks, kept, w_gate, w_up):
    outs = [jax.ShapeDtypeStruct((2 * scaled.shape[0], w_gate.shape[2]), jnp.bfloat16)]
    return half_columns(last_kernel, [scaled, marks], [VMEM] * 2, kept, w_gate, w_up, outs, "gate_up_last")[0]


def mix(a, b, scale, marks, experts, size):
    def both(start):
        return a[:, start : start + size].astype(jnp.float32) + b[:, start : start + size].astype(jnp.float32)

    rows = a.shape[0] // 2
    gate, up = both(0) * scale, both(size) * scale
    value = gate / (1.0 + jnp.exp(-gate)) * up
    return [
        (
            value[0:rows] * marks[0:rows, e : e + 1] + value[rows : 2 * rows] * marks[rows : 2 * rows, e : e + 1]
        ).astype(jnp.bfloat16)
        for e in range(experts)
    ]


def down_part(mixed, down, start, size, at):
    out = jnp.dot(mixed[0], down[0, start : start + size, at], preferred_element_type=jnp.float32)
    for e in range(1, len(mixed)):
        out = out + jnp.dot(mixed[e], down[e, start : start + size, at], preferred_element_type=jnp.float32)
    return out


def down_first_kernel(width, first, kept, a, b, marks, total, scales):
    (down,) = kept
    experts, _, depth = down.shape
    rows = a.shape[0] // 2
    at = slice(2 * first, 2 * first + 128)
    square = a[:, at].astype(jnp.float32) + b[:, at].astype(jnp.float32)
    scale = lax.rsqrt((square[0:rows] + square[rows : 2 * rows]) / width + epsilon)
    scale = jnp.concatenate([scale, scale], axis=0)
    scales[...] = scale
    mixed = mix(a, b, scale[:, 0:1], marks, experts, first)
    piece = depth // GROUP
    for n in range(GROUP):
        at = slice(n * piece, (n + 1) * piece)
        total[:, at] = down_part(mixed, down, 0, first, at)


def down_first(a, b, marks, down, width, first):
    experts, _, depth = down.shape
    rows = a.shape[0] // 2
    size = experts * first * depth
    return with_weights(
        functools.partial(down_first_kernel, width, first),
        [a, b, marks],
        [down],
        [VMEM] * 3,
        [
            jax.ShapeDtypeStruct((rows, depth), jnp.float32),
            jax.ShapeDtypeStruct((2 * rows, 128), jnp.float32),
        ],
        [],
        "down_first",
        flops=2 * rows * size,
        bytes_accessed=2 * size,
    )


def down_last_kernel(whole, first, kept, place, a, b, scales, before, marks, *refs):
    (down,) = kept
    outs, total = refs[:-1], refs[-1]
    experts, hidden, depth = down.shape
    rows = total.shape[0]
    mixed = mix(a, b, scales[:, 0:1], marks, experts, hidden - first)
    piece = depth // GROUP
    for n in range(GROUP):
        at = slice(n * piece, (n + 1) * piece)
        total[:, at] = before[:, at] + down_part(mixed, down, first, hidden - first, at)
    mine = place[0]
    for o in range(GROUP):
        if whole:
            matrix = rows_of(16, rows, lambda row: 8 * (row >> 1) + 2 * (mine ^ o) + (row & 1))
            outs[o][...] = pick(matrix, total[...])[0:8, :].astype(outs[o].dtype)
        else:
            at = pl.ds(pl.multiple_of((mine ^ o) * piece, 128), piece)
            outs[o][...] = total[:, at].astype(outs[o].dtype)


def down_last(place, a, b, scales, before, marks, down, first, whole):
    experts, hidden, depth = down.shape
    rows = a.shape[0] // 2
    size = experts * (hidden - first) * depth
    shape = (2 * GROUP, depth) if whole else (rows, depth // GROUP)
    shapes = [jax.ShapeDtypeStruct(shape, jnp.float32)]
    shapes += [jax.ShapeDtypeStruct(shape, jnp.bfloat16)] * (GROUP - 1)
    return with_weights(
        functools.partial(down_last_kernel, whole, first),
        [place, a, b, scales, before, marks],
        [down],
        [SMEM] + [VMEM] * 5,
        shapes,
        [pltpu.VMEM((rows, depth), jnp.float32)],
        "down_last",
        flops=2 * rows * size,
        bytes_accessed=2 * size,
    )


def swap(value, axis, offset):
    size = lax.axis_size(axis)
    return lax.ppermute(value, axis, [(i, i ^ offset) for i in range(size)])


def body(tokens, norm_gain, routes, route_weights, w_gate, w_up, w_down):
    steps, rows, top = routes.shape
    experts, depth, hidden = w_gate.shape
    width = depth * lax.axis_size("narrow")
    first = hidden // 2
    index = lax.axis_index("wide").astype(jnp.int32)
    place = jnp.stack([index % GROUP, index // GROUP, index])
    place, gain, marks = prepare(place, norm_gain, routes, route_weights, experts)

    def around(value, scale):
        return [value] + [swap(value, "wide", scale * o) for o in range(1, GROUP)]

    down, note = load_down(place, w_down)
    held, note = pack(note, around(tokens, GROUP))
    heads = load_heads(note, w_gate, w_up)
    pieces = split(place, around(held, 1))
    for step in range(steps):
        a1, scaled = first_columns(place, pieces, gain, marks[step], heads[0], w_gate, w_up)
        b1 = swap(a1, "narrow", 1)
        a2 = last_columns(scaled, marks[step], heads[1], w_gate, w_up)
        b2 = swap(a2, "narrow", 1)
        final = step == steps - 1
        before, scales = down_first(a1, b1, marks[step], down, width, first)
        parts = down_last(place, a2, b2, scales, before, marks[step], down, first, final)
        own = add_up([parts[0]] + [swap(parts[o], "wide", o) for o in range(1, GROUP)])
        sums = around(own, GROUP)
        if final:
            return finish(place, sums, pieces)
        pieces = around(add_up([pieces[0]] + sums), 1)


def plain_body(tokens, norm_gain, routes, route_weights, w_gate, w_up, w_down):
    experts = w_gate.shape[0]
    steps, rows, top = routes.shape
    width = tokens.shape[1] * lax.axis_size("narrow")
    gain = norm_gain.astype(jnp.float32)
    named = (routes[..., None] == jnp.arange(experts, dtype=jnp.int32)).astype(jnp.float32)
    current = tokens
    for step in range(steps):
        values = current.astype(jnp.float32)
        squares = lax.psum(jnp.sum(values * values, axis=1), "narrow")
        normed = (values * lax.rsqrt(squares[:, None] / width + epsilon) * gain[None, :]).astype(jnp.bfloat16)
        normed = lax.all_gather(normed, "wide", axis=0, tiled=True)
        gate = jnp.einsum("rd,edf->erf", normed, w_gate, preferred_element_type=jnp.float32)
        up = jnp.einsum("rd,edf->erf", normed, w_up, preferred_element_type=jnp.float32)
        gate = lax.psum(gate.astype(jnp.bfloat16), "narrow").astype(jnp.float32)
        up = lax.psum(up.astype(jnp.bfloat16), "narrow").astype(jnp.float32)
        value = (jax.nn.silu(gate) * up).astype(jnp.bfloat16)
        out = jnp.einsum("erf,efd->erd", value, w_down, preferred_element_type=jnp.float32)
        share = jnp.sum(named[step] * route_weights[step][..., None], axis=1)
        combined = jnp.einsum("re,erd->rd", share, out, precision=lax.Precision.HIGHEST)
        summed = lax.psum_scatter(combined, "wide", scatter_dimension=0, tiled=True)
        current = (current.astype(jnp.float32) + summed).astype(jnp.bfloat16)
    return current


def solution(mesh):
    placed = (
        P("wide", "narrow"),
        P("narrow"),
        P(),
        P(),
        P(None, "narrow", "wide"),
        P(None, "narrow", "wide"),
        P(None, "wide", "narrow"),
    )

    def call(*args):
        tokens, _, routes, _, w_gate, _, _ = args
        wide, narrow = mesh.shape["wide"], mesh.shape["narrow"]
        depth, hidden = w_gate.shape[1] // narrow, w_gate.shape[2] // wide
        routes = args[2]
        fits = narrow == 2 and wide == GROUP * GROUP and routes.shape[2] == 2 and w_gate.shape[0] >= 2
        fits = fits and depth % (GROUP * 128) == 0 and hidden % 512 == 0 and routes.shape[1] == 2 * GROUP * GROUP
        return jax.shard_map(
            body if fits else plain_body, mesh=mesh, in_specs=placed, out_specs=P("wide", "narrow"), check_vma=False
        )(*args)

    return call
```

```python
import functools

import jax
import jax.numpy as jnp
from jax import lax
from jax.experimental import pallas as pl
from jax.experimental.pallas import tpu as pltpu
from jax.sharding import PartitionSpec as P

epsilon = 1e-05
MIB = 1 << 20
VMEM = pl.BlockSpec(memory_space=pltpu.VMEM)
HBM = pl.BlockSpec(memory_space=pltpu.HBM)
GROUP = 4
SLOTS = 4
KEPT = 2
NOTE = jax.ShapeDtypeStruct((8, 128), jnp.float32)
LIMIT = 2 * MIB
FIRST_LIMIT = 8 * MIB


def in_vmem(array):
    return pltpu.with_memory_space_constraint(array, pltpu.VMEM)


def in_hbm(array):
    return pltpu.with_memory_space_constraint(array, pltpu.HBM)


def with_weights(kernel, inputs, kept, specs, shapes, scratch, name, limit=None, **cost):
    count = len(inputs)

    def run(*refs):
        kernel(refs[count : count + len(kept)], *refs[:count], *refs[count + len(kept) :])

    more = {"cost_estimate": pl.CostEstimate(transcendentals=0, **cost)} if cost else {}
    return pl.pallas_call(
        run,
        in_specs=specs + [VMEM] * len(kept),
        out_specs=[VMEM] * len(shapes),
        out_shape=shapes,
        scratch_shapes=scratch,
        name=name,
        compiler_params=pltpu.CompilerParams(vmem_limit_bytes=limit or LIMIT),
        **more,
    )(*inputs, *[in_vmem(weight) for weight in kept])


def where():
    index = lax.axis_index("wide")
    return lax.rem(index, GROUP), lax.div(index, GROUP), index


def prepare_kernel(gain, named, weight, gain_out, note, *marks):
    note[...] = jnp.zeros_like(note)
    gain_out[...] = gain[...].astype(jnp.float32)
    for step, mark in enumerate(marks):
        column = lax.broadcasted_iota(jnp.int32, mark.shape, 1)
        experts = mark.shape[1] // 2
        expert = jnp.where(column < experts, column, column - experts)
        value = jnp.where(column < experts, weight[step], 1.0)
        mark[...] = jnp.where(named[step] == expert, value, 0.0)


def prepare(gain, routes, route_weights, experts):
    steps, rows, top = routes.shape
    named = jnp.swapaxes(routes, 1, 2).reshape(steps, top * rows, 1)
    weight = jnp.swapaxes(route_weights, 1, 2).reshape(steps, top * rows, 1)
    gain, note, *marks = pl.pallas_call(
        prepare_kernel,
        in_specs=[VMEM] * 3,
        out_specs=[VMEM] * (2 + steps),
        out_shape=[jax.ShapeDtypeStruct((1, gain.shape[0]), jnp.float32), NOTE]
        + [jax.ShapeDtypeStruct((top * rows, 2 * experts), jnp.float32)] * steps,
        name="prepare",
        compiler_params=pltpu.CompilerParams(vmem_limit_bytes=4 * MIB),
    )(gain.reshape(1, -1), named, weight)
    return note, gain, marks


def pack_kernel(note, a, b, c, d, out, note_out, rows):
    note_out[...] = note[...]
    for k, ref in enumerate((a, b, c, d)):
        rows[2 * k : 2 * k + 2, :] = ref[...].astype(jnp.float32)
    out[...] = rows[...].astype(out.dtype)


def pack(note, parts):
    depth = parts[0].shape[1]
    return pl.pallas_call(
        pack_kernel,
        in_specs=[VMEM] * 5,
        out_specs=[VMEM] * 2,
        out_shape=[jax.ShapeDtypeStruct((8, depth), jnp.bfloat16), NOTE],
        scratch_shapes=[pltpu.VMEM((8, depth), jnp.float32)],
        name="pack",
        compiler_params=pltpu.CompilerParams(vmem_limit_bytes=MIB),
    )(note, *parts)


def rows_of(count, all_rows, wanted):
    row = lax.broadcasted_iota(jnp.int32, (count, all_rows), 0)
    column = lax.broadcasted_iota(jnp.int32, (count, all_rows), 1)
    return jnp.where(wanted(row) == column, 1.0, 0.0).astype(jnp.bfloat16)


def pick(matrix, rows):
    return jnp.dot(matrix, rows.astype(jnp.bfloat16), preferred_element_type=jnp.float32)


def split_kernel(_, a, b, c, d, *refs):
    outs, rows = refs[:-1], refs[-1]
    mine, line, _ = where()
    for o, ref in enumerate((a, b, c, d)):
        rows[8 * o : 8 * o + 8, :] = ref[...].astype(jnp.float32)

    def source(row):
        return 8 * (((row >> 1) & 3) ^ mine) + 2 * ((row >> 3) ^ line) + (row & 1)

    count = rows.shape[0]
    rows[...] = pick(rows_of(count, count, source), rows[...])
    piece = outs[0].shape[1]
    for o in range(GROUP):
        at = pl.ds(pl.multiple_of((mine ^ o) * piece, 128), piece)
        outs[o][...] = rows[:, at].astype(jnp.bfloat16)


def split(parts):
    depth = parts[0].shape[1]
    rows = GROUP * parts[0].shape[0]
    return with_weights(
        split_kernel,
        parts,
        [],
        [VMEM] * 4,
        [jax.ShapeDtypeStruct((rows, depth // GROUP), jnp.bfloat16)] * GROUP,
        [pltpu.VMEM((rows, depth), jnp.float32)],
        "split",
    )


def sum_kernel(_, *refs):
    total = refs[0][...].astype(jnp.float32)
    for ref in refs[1:-1]:
        total = total + ref[...].astype(jnp.float32)
    refs[-1][...] = total.astype(refs[-1].dtype)


def add_up(parts):
    shapes = [jax.ShapeDtypeStruct(parts[0].shape, jnp.bfloat16)]
    return with_weights(sum_kernel, parts, [], [VMEM] * len(parts), shapes, [], "add_up")[0]


def finish_kernel(_, s0, s1, s2, s3, x0, x1, x2, x3, out, rows, total):
    mine, line, index = where()
    for k, ref in enumerate((s0, s1, s2, s3)):
        total[8 * k : 8 * k + 8, :] = ref[...].astype(jnp.float32)
    piece = x0.shape[1]
    for o, ref in enumerate((x0, x1, x2, x3)):
        at = pl.ds(pl.multiple_of((mine ^ o) * piece, 128), piece)
        rows[:, at] = ref[...].astype(jnp.float32)
    count = rows.shape[0]
    result = pick(rows_of(16, count, lambda row: 2 * index + row), rows[...])
    for k in range(GROUP):
        result = result + pick(rows_of(16, count, lambda row: 8 * k + 2 * line + row), total[...])
    out[...] = result[0:2, :].astype(out.dtype)


def finish(sums, pieces):
    depth = sums[0].shape[1]
    rows = pieces[0].shape[0]
    return with_weights(
        finish_kernel,
        [*sums, *pieces],
        [],
        [VMEM] * 8,
        [jax.ShapeDtypeStruct((2, depth), jnp.bfloat16)],
        [pltpu.VMEM((rows, depth), jnp.float32)] * 2,
        "finish",
    )[0]


def load_down_kernel(before, w_down, down, note, sem):
    del before
    copies = [pltpu.make_async_copy(w_down.at[e], down.at[e], sem.at[e]) for e in range(w_down.shape[0])]
    for copy in copies:
        copy.start()
    note[...] = jnp.zeros_like(note)
    for copy in copies:
        copy.wait()


def load_down(note, w_down):
    return pl.pallas_call(
        load_down_kernel,
        in_specs=[VMEM, HBM],
        out_specs=[VMEM] * 2,
        out_shape=[pltpu.VMEM(w_down.shape, w_down.dtype), NOTE],
        scratch_shapes=[pltpu.SemaphoreType.DMA((w_down.shape[0],))],
        name="load_down",
        cost_estimate=pl.CostEstimate(flops=0, bytes_accessed=2 * w_down.size, transcendentals=0),
        compiler_params=pltpu.CompilerParams(vmem_limit_bytes=LIMIT),
    )(note, in_hbm(w_down))


def load_heads_kernel(note, w_gate, w_up, *refs):
    del note
    heads, sem = refs[:-1], refs[-1]
    half = w_gate.shape[2] // len(heads)
    copies = []
    for c, head in enumerate(heads):
        for e in range(head.shape[0]):
            for m, weight in enumerate((w_gate, w_up)):
                copies.append(
                    pltpu.make_async_copy(
                        weight.at[e, :, pl.ds(c * half, half)],
                        head.at[e, :, pl.ds(m * half, half)],
                        sem.at[len(copies)],
                    )
                )
    for copy in copies:
        copy.start()
    for copy in copies:
        copy.wait()


def load_heads(note, w_gate, w_up):
    _, depth, hidden = w_gate.shape
    head = pltpu.VMEM((KEPT, depth, hidden), w_gate.dtype)
    return pl.pallas_call(
        load_heads_kernel,
        in_specs=[VMEM] + [HBM] * 2,
        out_specs=[VMEM] * 2,
        out_shape=[head, head],
        scratch_shapes=[pltpu.SemaphoreType.DMA((4 * KEPT,))],
        name="load_heads",
        cost_estimate=pl.CostEstimate(flops=0, bytes_accessed=24 * MIB, transcendentals=0),
        compiler_params=pltpu.CompilerParams(vmem_limit_bytes=LIMIT),
    )(note, in_hbm(w_gate), in_hbm(w_up))


def scale_up(pieces, gain, scaled, chosen, start):
    rows, piece = pieces[0].shape
    mine, _, _ = where()
    square = jnp.zeros((rows, 1), jnp.float32)
    for o, ref in enumerate(pieces):
        at = pl.ds(pl.multiple_of((mine ^ o) * piece, 128), piece)
        values = ref[...].astype(jnp.float32)
        square = square + jnp.sum(values * values, axis=1, keepdims=True)
        scaled[:, at] = (values * gain[:, at]).astype(jnp.bfloat16)
    coarse = square.astype(jnp.bfloat16)
    fine = (square - coarse.astype(jnp.float32)).astype(jnp.bfloat16)
    chosen[0:rows, start : start + 128] = jnp.broadcast_to(coarse, (rows, 128))
    chosen[rows : 2 * rows, start : start + 128] = jnp.broadcast_to(fine, (rows, 128))


def half_product(start, kept, scaled, marks, w_gate, w_up, chosen, ring, total, sem, before=None):
    (head,) = kept
    experts, depth, _ = w_gate.shape
    half = ring.shape[2] // 2
    rows = total.shape[1]
    block = ring.shape[1]
    streamed = [(e, q) for e in range(head.shape[0], experts) for q in range(depth // block)]
    resident = [(e, q) for e in range(head.shape[0]) for q in range(depth // block)]

    def copies(i):
        e, q = streamed[i]
        slot = i % SLOTS
        return [
            pltpu.make_async_copy(
                weight.at[e, pl.ds(q * block, block), pl.ds(start, half)],
                ring.at[slot, :, pl.ds(m * half, half)],
                sem.at[slot, m],
            )
            for m, weight in enumerate((w_gate, w_up))
        ]

    for i in range(min(SLOTS, len(streamed))):
        for copy in copies(i):
            copy.start()
    if before is not None:
        before()

    def add(e, q, weight):
        product = jnp.dot(
            scaled[:, q * block : (q + 1) * block], weight, preferred_element_type=jnp.float32
        )
        if q:
            total[e] += product
        else:
            total[e] = product

    ahead = max(len(resident) - len(streamed) // 2 + 1, 0)
    for i in range(ahead):
        e, q = resident[i]
        add(e, q, head[e, q * block : (q + 1) * block, :])
    left = resident[ahead:]
    for i in range(len(streamed)):
        for copy in copies(i):
            copy.wait()
        add(*streamed[i], ring[i % SLOTS])
        if i + SLOTS < len(streamed):
            for copy in copies(i + SLOTS):
                copy.start()
        if left and (i % 2 == 1 or i + 1 == len(streamed)):
            for e, q in left if i + 1 == len(streamed) else left[:1]:
                add(e, q, head[e, q * block : (q + 1) * block, :])
            left = left[1:]
    for k in range(2):
        picked = jnp.zeros((rows, 2 * half), jnp.float32)
        for e in range(experts):
            mark = marks[k * rows : (k + 1) * rows, experts + e : experts + e + 1]
            picked = jnp.where(mark > 0, total[e], picked)
        chosen[k * rows : (k + 1) * rows, 0 : 2 * half] = picked.astype(jnp.bfloat16)


def first_kernel(kept, x0, x1, x2, x3, gain, marks, w_gate, w_up, chosen, scaled, ring, total, sem):
    half_product(
        0, kept, scaled, marks, w_gate, w_up, chosen, ring, total, sem,
        before=lambda: scale_up((x0, x1, x2, x3), gain, scaled, chosen, ring.shape[2]),
    )


def last_kernel(kept, scaled, marks, w_gate, w_up, chosen, ring, total, sem):
    half_product(ring.shape[2] // 2, kept, scaled, marks, w_gate, w_up, chosen, ring, total, sem)


def half_columns(kernel, inputs, specs, kept, w_gate, w_up, outs, name):
    experts, depth, hidden = w_gate.shape
    rows = outs[0].shape[0] // 2
    count = experts * depth * hidden
    return with_weights(
        kernel,
        [*inputs, in_hbm(w_gate), in_hbm(w_up)],
        [kept],
        specs + [HBM] * 2,
        outs,
        [
            pltpu.VMEM((SLOTS, depth // GROUP, hidden), jnp.bfloat16),
            pltpu.VMEM((experts, rows, hidden), jnp.float32),
            pltpu.SemaphoreType.DMA((SLOTS, 2)),
        ],
        name,
        limit=FIRST_LIMIT,
        flops=2 * rows * count,
        bytes_accessed=2 * count,
    )


def first_columns(pieces, gain, marks, kept, w_gate, w_up):
    _, depth, hidden = w_gate.shape
    rows = pieces[0].shape[0]
    outs = [
        jax.ShapeDtypeStruct((2 * rows, hidden + 128), jnp.bfloat16),
        jax.ShapeDtypeStruct((rows, depth), jnp.bfloat16),
    ]
    return half_columns(
        first_kernel, [*pieces, gain, marks], [VMEM] * 6, kept, w_gate, w_up, outs, "gate_up_first"
    )


def last_columns(scaled, marks, kept, w_gate, w_up):
    outs = [jax.ShapeDtypeStruct((2 * scaled.shape[0], w_gate.shape[2]), jnp.bfloat16)]
    return half_columns(last_kernel, [scaled, marks], [VMEM] * 2, kept, w_gate, w_up, outs, "gate_up_last")[0]


def mix(a, b, scale, marks, experts, size):
    def both(start):
        return a[:, start : start + size].astype(jnp.float32) + b[:, start : start + size].astype(jnp.float32)

    rows = a.shape[0] // 2
    gate, up = both(0) * scale, both(size) * scale
    value = gate / (1.0 + jnp.exp(-gate)) * up
    return [
        (
            value[0:rows] * marks[0:rows, e : e + 1] + value[rows : 2 * rows] * marks[rows : 2 * rows, e : e + 1]
        ).astype(jnp.bfloat16)
        for e in range(experts)
    ]


def down_part(mixed, down, start, size, at):
    out = jnp.dot(mixed[0], down[0, start : start + size, at], preferred_element_type=jnp.float32)
    for e in range(1, len(mixed)):
        out = out + jnp.dot(mixed[e], down[e, start : start + size, at], preferred_element_type=jnp.float32)
    return out


def down_first_kernel(width, first, kept, a, b, marks, total, scales):
    (down,) = kept
    experts, _, depth = down.shape
    rows = a.shape[0] // 2
    at = slice(2 * first, 2 * first + 128)
    square = a[:, at].astype(jnp.float32) + b[:, at].astype(jnp.float32)
    scale = lax.rsqrt((square[0:rows] + square[rows : 2 * rows]) / width + epsilon)
    scale = jnp.concatenate([scale, scale], axis=0)
    scales[...] = scale
    mixed = mix(a, b, scale[:, 0:1], marks, experts, first)
    piece = depth // GROUP
    for n in range(GROUP):
        at = slice(n * piece, (n + 1) * piece)
        total[:, at] = down_part(mixed, down, 0, first, at)


def down_first(a, b, marks, down, width, first):
    experts, _, depth = down.shape
    rows = a.shape[0] // 2
    size = experts * first * depth
    return with_weights(
        functools.partial(down_first_kernel, width, first),
        [a, b, marks],
        [down],
        [VMEM] * 3,
        [
            jax.ShapeDtypeStruct((rows, depth), jnp.float32),
            jax.ShapeDtypeStruct((2 * rows, 128), jnp.float32),
        ],
        [],
        "down_first",
        flops=2 * rows * size,
        bytes_accessed=2 * size,
    )


def down_last_kernel(whole, first, kept, a, b, scales, before, marks, *refs):
    (down,) = kept
    outs, total = refs[:-1], refs[-1]
    experts, hidden, depth = down.shape
    rows = total.shape[0]
    mixed = mix(a, b, scales[:, 0:1], marks, experts, hidden - first)
    piece = depth // GROUP
    for n in range(GROUP):
        at = slice(n * piece, (n + 1) * piece)
        total[:, at] = before[:, at] + down_part(mixed, down, first, hidden - first, at)
    mine, _, _ = where()
    for o in range(GROUP):
        if whole:
            matrix = rows_of(16, rows, lambda row: 8 * (row >> 1) + 2 * (mine ^ o) + (row & 1))
            outs[o][...] = pick(matrix, total[...])[0:8, :].astype(outs[o].dtype)
        else:
            at = pl.ds(pl.multiple_of((mine ^ o) * piece, 128), piece)
            outs[o][...] = total[:, at].astype(outs[o].dtype)


def down_last(a, b, scales, before, marks, down, first, whole):
    experts, hidden, depth = down.shape
    rows = a.shape[0] // 2
    size = experts * (hidden - first) * depth
    shape = (2 * GROUP, depth) if whole else (rows, depth // GROUP)
    shapes = [jax.ShapeDtypeStruct(shape, jnp.float32)]
    shapes += [jax.ShapeDtypeStruct(shape, jnp.bfloat16)] * (GROUP - 1)
    return with_weights(
        functools.partial(down_last_kernel, whole, first),
        [a, b, scales, before, marks],
        [down],
        [VMEM] * 5,
        shapes,
        [pltpu.VMEM((rows, depth), jnp.float32)],
        "down_last",
        flops=2 * rows * size,
        bytes_accessed=2 * size,
    )


def swap(value, axis, offset):
    size = lax.axis_size(axis)
    return lax.ppermute(value, axis, [(i, i ^ offset) for i in range(size)])


def body(tokens, norm_gain, routes, route_weights, w_gate, w_up, w_down):
    steps, rows, top = routes.shape
    experts, depth, hidden = w_gate.shape
    width = depth * lax.axis_size("narrow")
    first = hidden // 2
    note, gain, marks = prepare(norm_gain, routes, route_weights, experts)

    def around(value, scale):
        return [value] + [swap(value, "wide", scale * o) for o in range(1, GROUP)]

    down, note = load_down(note, w_down)
    held, note = pack(note, around(tokens, GROUP))
    heads = load_heads(note, w_gate, w_up)
    pieces = split(around(held, 1))
    for step in range(steps):
        a1, scaled = first_columns(pieces, gain, marks[step], heads[0], w_gate, w_up)
        b1 = swap(a1, "narrow", 1)
        a2 = last_columns(scaled, marks[step], heads[1], w_gate, w_up)
        b2 = swap(a2, "narrow", 1)
        final = step == steps - 1
        before, scales = down_first(a1, b1, marks[step], down, width, first)
        parts = down_last(a2, b2, scales, before, marks[step], down, first, final)
        own = add_up([parts[0]] + [swap(parts[o], "wide", o) for o in range(1, GROUP)])
        sums = around(own, GROUP)
        if final:
            return finish(sums, pieces)
        pieces = around(add_up([pieces[0]] + sums), 1)


def plain_body(tokens, norm_gain, routes, route_weights, w_gate, w_up, w_down):
    experts = w_gate.shape[0]
    steps, rows, top = routes.shape
    width = tokens.shape[1] * lax.axis_size("narrow")
    gain = norm_gain.astype(jnp.float32)
    named = (routes[..., None] == jnp.arange(experts, dtype=jnp.int32)).astype(jnp.float32)
    current = tokens
    for step in range(steps):
        values = current.astype(jnp.float32)
        squares = lax.psum(jnp.sum(values * values, axis=1), "narrow")
        normed = (values * lax.rsqrt(squares[:, None] / width + epsilon) * gain[None, :]).astype(jnp.bfloat16)
        normed = lax.all_gather(normed, "wide", axis=0, tiled=True)
        gate = jnp.einsum("rd,edf->erf", normed, w_gate, preferred_element_type=jnp.float32)
        up = jnp.einsum("rd,edf->erf", normed, w_up, preferred_element_type=jnp.float32)
        gate = lax.psum(gate.astype(jnp.bfloat16), "narrow").astype(jnp.float32)
        up = lax.psum(up.astype(jnp.bfloat16), "narrow").astype(jnp.float32)
        value = (jax.nn.silu(gate) * up).astype(jnp.bfloat16)
        out = jnp.einsum("erf,efd->erd", value, w_down, preferred_element_type=jnp.float32)
        share = jnp.sum(named[step] * route_weights[step][..., None], axis=1)
        combined = jnp.einsum("re,erd->rd", share, out, precision=lax.Precision.HIGHEST)
        summed = lax.psum_scatter(combined, "wide", scatter_dimension=0, tiled=True)
        current = (current.astype(jnp.float32) + summed).astype(jnp.bfloat16)
    return current


def solution(mesh):
    placed = (
        P("wide", "narrow"),
        P("narrow"),
        P(),
        P(),
        P(None, "narrow", "wide"),
        P(None, "narrow", "wide"),
        P(None, "wide", "narrow"),
    )

    def call(*args):
        tokens, _, routes, _, w_gate, _, _ = args
        wide, narrow = mesh.shape["wide"], mesh.shape["narrow"]
        depth, hidden = w_gate.shape[1] // narrow, w_gate.shape[2] // wide
        routes = args[2]
        fits = narrow == 2 and wide == GROUP * GROUP and routes.shape[2] == 2 and w_gate.shape[0] >= 2
        fits = fits and depth % (GROUP * 128) == 0 and hidden % 512 == 0 and routes.shape[1] == 2 * GROUP * GROUP
        return jax.shard_map(
            body if fits else plain_body, mesh=mesh, in_specs=placed, out_specs=P("wide", "narrow"), check_vma=False
        )(*args)

    return call
```

```python
import functools

import jax
import jax.numpy as jnp
from jax import lax
from jax.experimental import pallas as pl
from jax.experimental.pallas import tpu as pltpu
from jax.sharding import PartitionSpec as P

epsilon = 1e-05
MIB = 1 << 20
VMEM = pl.BlockSpec(memory_space=pltpu.VMEM)
HBM = pl.BlockSpec(memory_space=pltpu.HBM)
GROUP = 4
SLOTS = 4
KEPT = 2
NOTE = jax.ShapeDtypeStruct((8, 128), jnp.float32)
LIMIT = 2 * MIB
FIRST_LIMIT = 8 * MIB


def in_vmem(array):
    return pltpu.with_memory_space_constraint(array, pltpu.VMEM)


def in_hbm(array):
    return pltpu.with_memory_space_constraint(array, pltpu.HBM)


def with_weights(kernel, inputs, kept, specs, shapes, scratch, name, limit=None, **cost):
    count = len(inputs)

    def run(*refs):
        kernel(refs[count : count + len(kept)], *refs[:count], *refs[count + len(kept) :])

    more = {"cost_estimate": pl.CostEstimate(transcendentals=0, **cost)} if cost else {}
    return pl.pallas_call(
        run,
        in_specs=specs + [VMEM] * len(kept),
        out_specs=[VMEM] * len(shapes),
        out_shape=shapes,
        scratch_shapes=scratch,
        name=name,
        compiler_params=pltpu.CompilerParams(vmem_limit_bytes=limit or LIMIT),
        **more,
    )(*inputs, *[in_vmem(weight) for weight in kept])


def where():
    index = lax.axis_index("wide")
    return lax.rem(index, GROUP), lax.div(index, GROUP), index


def prepare_kernel(gain, named, weight, gain_out, note, *marks):
    note[...] = jnp.zeros_like(note)
    gain_out[...] = gain[...].astype(jnp.float32).reshape(gain_out.shape)
    steps, top, rows = named.shape
    same = lax.broadcasted_iota(jnp.int32, (rows, rows), 0) == lax.broadcasted_iota(jnp.int32, (rows, rows), 1)
    for step, mark in enumerate(marks):
        experts = mark.shape[1] // 2
        column = lax.broadcasted_iota(jnp.int32, (rows, 2 * experts), 1)
        expert = jnp.where(column < experts, column, column - experts)
        for k in range(top):
            chosen = jnp.sum(jnp.where(same, named[step, k : k + 1, :], 0), axis=1, keepdims=True)
            scale = jnp.sum(jnp.where(same, weight[step, k : k + 1, :], 0.0), axis=1, keepdims=True)
            value = jnp.where(column < experts, scale, 1.0)
            mark[k * rows : (k + 1) * rows, :] = jnp.where(chosen == expert, value, 0.0)


def prepare(gain, routes, route_weights, experts):
    steps, rows, top = routes.shape
    gain, note, *marks = pl.pallas_call(
        prepare_kernel,
        in_specs=[VMEM] * 3,
        out_specs=[VMEM] * (2 + steps),
        out_shape=[jax.ShapeDtypeStruct((1, gain.shape[0]), jnp.float32), NOTE]
        + [jax.ShapeDtypeStruct((top * rows, 2 * experts), jnp.float32)] * steps,
        name="prepare",
        compiler_params=pltpu.CompilerParams(vmem_limit_bytes=4 * MIB),
    )(in_hbm(gain), in_hbm(jnp.swapaxes(routes, 1, 2)), in_hbm(jnp.swapaxes(route_weights, 1, 2)))
    return note, gain, marks


def pack_kernel(note, a, b, c, d, out, note_out, rows):
    note_out[...] = note[...]
    for k, ref in enumerate((a, b, c, d)):
        rows[2 * k : 2 * k + 2, :] = ref[...].astype(jnp.float32)
    out[...] = rows[...].astype(out.dtype)


def pack(note, parts):
    depth = parts[0].shape[1]
    return pl.pallas_call(
        pack_kernel,
        in_specs=[VMEM] * 5,
        out_specs=[VMEM] * 2,
        out_shape=[jax.ShapeDtypeStruct((8, depth), jnp.bfloat16), NOTE],
        scratch_shapes=[pltpu.VMEM((8, depth), jnp.float32)],
        name="pack",
        compiler_params=pltpu.CompilerParams(vmem_limit_bytes=MIB),
    )(note, *parts)


def rows_of(count, all_rows, wanted):
    row = lax.broadcasted_iota(jnp.int32, (count, all_rows), 0)
    column = lax.broadcasted_iota(jnp.int32, (count, all_rows), 1)
    return jnp.where(wanted(row) == column, 1.0, 0.0).astype(jnp.bfloat16)


def pick(matrix, rows):
    return jnp.dot(matrix, rows.astype(jnp.bfloat16), preferred_element_type=jnp.float32)


def split_kernel(_, a, b, c, d, *refs):
    outs, rows = refs[:-1], refs[-1]
    mine, line, _ = where()
    for o, ref in enumerate((a, b, c, d)):
        rows[8 * o : 8 * o + 8, :] = ref[...].astype(jnp.float32)

    def source(row):
        return 8 * (((row >> 1) & 3) ^ mine) + 2 * ((row >> 3) ^ line) + (row & 1)

    count = rows.shape[0]
    rows[...] = pick(rows_of(count, count, source), rows[...])
    piece = outs[0].shape[1]
    for o in range(GROUP):
        at = pl.ds(pl.multiple_of((mine ^ o) * piece, 128), piece)
        outs[o][...] = rows[:, at].astype(jnp.bfloat16)


def split(parts):
    depth = parts[0].shape[1]
    rows = GROUP * parts[0].shape[0]
    return with_weights(
        split_kernel,
        parts,
        [],
        [VMEM] * 4,
        [jax.ShapeDtypeStruct((rows, depth // GROUP), jnp.bfloat16)] * GROUP,
        [pltpu.VMEM((rows, depth), jnp.float32)],
        "split",
    )


def sum_kernel(_, *refs):
    total = refs[0][...].astype(jnp.float32)
    for ref in refs[1:-1]:
        total = total + ref[...].astype(jnp.float32)
    refs[-1][...] = total.astype(refs[-1].dtype)


def add_up(parts):
    shapes = [jax.ShapeDtypeStruct(parts[0].shape, jnp.bfloat16)]
    return with_weights(sum_kernel, parts, [], [VMEM] * len(parts), shapes, [], "add_up")[0]


def finish_kernel(_, s0, s1, s2, s3, x0, x1, x2, x3, out, rows, total):
    mine, line, index = where()
    for k, ref in enumerate((s0, s1, s2, s3)):
        total[8 * k : 8 * k + 8, :] = ref[...].astype(jnp.float32)
    piece = x0.shape[1]
    for o, ref in enumerate((x0, x1, x2, x3)):
        at = pl.ds(pl.multiple_of((mine ^ o) * piece, 128), piece)
        rows[:, at] = ref[...].astype(jnp.float32)
    count = rows.shape[0]
    result = pick(rows_of(16, count, lambda row: 2 * index + row), rows[...])
    for k in range(GROUP):
        result = result + pick(rows_of(16, count, lambda row: 8 * k + 2 * line + row), total[...])
    out[...] = result[0:2, :].astype(out.dtype)


def finish(sums, pieces):
    depth = sums[0].shape[1]
    rows = pieces[0].shape[0]
    return with_weights(
        finish_kernel,
        [*sums, *pieces],
        [],
        [VMEM] * 8,
        [jax.ShapeDtypeStruct((2, depth), jnp.bfloat16)],
        [pltpu.VMEM((rows, depth), jnp.float32)] * 2,
        "finish",
    )[0]


def load_head_kernel(c, before, w_gate, w_up, head, note, sem):
    del before
    half = head.shape[2] // 2
    copies = []
    for e in range(head.shape[0]):
        for m, weight in enumerate((w_gate, w_up)):
            copies.append(
                pltpu.make_async_copy(
                    weight.at[e, :, pl.ds(c * half, half)],
                    head.at[e, :, pl.ds(m * half, half)],
                    sem.at[len(copies)],
                )
            )
    for copy in copies:
        copy.start()
    note[...] = jnp.zeros_like(note)
    for copy in copies:
        copy.wait()


def load_head(note, w_gate, w_up, c):
    _, depth, hidden = w_gate.shape
    return pl.pallas_call(
        functools.partial(load_head_kernel, c),
        in_specs=[VMEM] + [HBM] * 2,
        out_specs=[VMEM] * 2,
        out_shape=[pltpu.VMEM((KEPT, depth, hidden), w_gate.dtype), NOTE],
        scratch_shapes=[pltpu.SemaphoreType.DMA((2 * KEPT,))],
        name="load_head",
        cost_estimate=pl.CostEstimate(flops=0, bytes_accessed=12 * MIB, transcendentals=0),
        compiler_params=pltpu.CompilerParams(vmem_limit_bytes=LIMIT),
    )(note, in_hbm(w_gate), in_hbm(w_up))


def scale_up(pieces, gain, scaled, chosen, start):
    rows, piece = pieces[0].shape
    mine, _, _ = where()
    square = jnp.zeros((rows, 1), jnp.float32)
    for o, ref in enumerate(pieces):
        at = pl.ds(pl.multiple_of((mine ^ o) * piece, 128), piece)
        values = ref[...].astype(jnp.float32)
        square = square + jnp.sum(values * values, axis=1, keepdims=True)
        scaled[:, at] = (values * gain[:, at]).astype(jnp.bfloat16)
    coarse = square.astype(jnp.bfloat16)
    fine = (square - coarse.astype(jnp.float32)).astype(jnp.bfloat16)
    chosen[0:rows, start : start + 128] = jnp.broadcast_to(coarse, (rows, 128))
    chosen[rows : 2 * rows, start : start + 128] = jnp.broadcast_to(fine, (rows, 128))


def half_product(start, kept, scaled, marks, w_gate, w_up, chosen, ring, total, sem, before=None):
    (head,) = kept
    experts, depth, _ = w_gate.shape
    half = ring.shape[2] // 2
    rows = total.shape[1]
    block = ring.shape[1]
    streamed = [(e, q) for e in range(head.shape[0], experts) for q in range(depth // block)]
    resident = [(e, q) for e in range(head.shape[0]) for q in range(depth // block)]

    def copies(i):
        e, q = streamed[i]
        slot = i % SLOTS
        return [
            pltpu.make_async_copy(
                weight.at[e, pl.ds(q * block, block), pl.ds(start, half)],
                ring.at[slot, :, pl.ds(m * half, half)],
                sem.at[slot, m],
            )
            for m, weight in enumerate((w_gate, w_up))
        ]

    for i in range(min(SLOTS, len(streamed))):
        for copy in copies(i):
            copy.start()
    if before is not None:
        before()

    def add(e, q, weight):
        product = jnp.dot(
            scaled[:, q * block : (q + 1) * block], weight, preferred_element_type=jnp.float32
        )
        if q:
            total[e] += product
        else:
            total[e] = product

    ahead = max(len(resident) - len(streamed) // 2 + 1, 0)
    for i in range(ahead):
        e, q = resident[i]
        add(e, q, head[e, q * block : (q + 1) * block, :])
    left = resident[ahead:]
    for i in range(len(streamed)):
        for copy in copies(i):
            copy.wait()
        add(*streamed[i], ring[i % SLOTS])
        if i + SLOTS < len(streamed):
            for copy in copies(i + SLOTS):
                copy.start()
        if left and (i % 2 == 1 or i + 1 == len(streamed)):
            for e, q in left if i + 1 == len(streamed) else left[:1]:
                add(e, q, head[e, q * block : (q + 1) * block, :])
            left = left[1:]
    for k in range(2):
        picked = jnp.zeros((rows, 2 * half), jnp.float32)
        for e in range(experts):
            mark = marks[k * rows : (k + 1) * rows, experts + e : experts + e + 1]
            picked = jnp.where(mark > 0, total[e], picked)
        chosen[k * rows : (k + 1) * rows, 0 : 2 * half] = picked.astype(jnp.bfloat16)


def first_kernel(kept, x0, x1, x2, x3, gain, marks, w_gate, w_up, chosen, scaled, ring, total, sem):
    half_product(
        0, kept, scaled, marks, w_gate, w_up, chosen, ring, total, sem,
        before=lambda: scale_up((x0, x1, x2, x3), gain, scaled, chosen, ring.shape[2]),
    )


def last_kernel(kept, scaled, marks, w_gate, w_up, chosen, ring, total, sem):
    half_product(ring.shape[2] // 2, kept, scaled, marks, w_gate, w_up, chosen, ring, total, sem)


def half_columns(kernel, inputs, specs, kept, w_gate, w_up, outs, name):
    experts, depth, hidden = w_gate.shape
    rows = outs[0].shape[0] // 2
    count = experts * depth * hidden
    return with_weights(
        kernel,
        [*inputs, in_hbm(w_gate), in_hbm(w_up)],
        [kept],
        specs + [HBM] * 2,
        outs,
        [
            pltpu.VMEM((SLOTS, depth // GROUP, hidden), jnp.bfloat16),
            pltpu.VMEM((experts, rows, hidden), jnp.float32),
            pltpu.SemaphoreType.DMA((SLOTS, 2)),
        ],
        name,
        limit=FIRST_LIMIT,
        flops=2 * rows * count,
        bytes_accessed=2 * count,
    )


def first_columns(pieces, gain, marks, kept, w_gate, w_up):
    _, depth, hidden = w_gate.shape
    rows = pieces[0].shape[0]
    outs = [
        jax.ShapeDtypeStruct((2 * rows, hidden + 128), jnp.bfloat16),
        jax.ShapeDtypeStruct((rows, depth), jnp.bfloat16),
    ]
    return half_columns(
        first_kernel, [*pieces, gain, marks], [VMEM] * 6, kept, w_gate, w_up, outs, "gate_up_first"
    )


def last_columns(scaled, marks, kept, w_gate, w_up):
    outs = [jax.ShapeDtypeStruct((2 * scaled.shape[0], w_gate.shape[2]), jnp.bfloat16)]
    return half_columns(last_kernel, [scaled, marks], [VMEM] * 2, kept, w_gate, w_up, outs, "gate_up_last")[0]


def mix(a, b, scale, marks, experts, size):
    def both(start):
        return a[:, start : start + size].astype(jnp.float32) + b[:, start : start + size].astype(jnp.float32)

    rows = a.shape[0] // 2
    gate, up = both(0) * scale, both(size) * scale
    value = gate / (1.0 + jnp.exp(-gate)) * up
    return [
        (
            value[0:rows] * marks[0:rows, e : e + 1] + value[rows : 2 * rows] * marks[rows : 2 * rows, e : e + 1]
        ).astype(jnp.bfloat16)
        for e in range(experts)
    ]


def down_part(mixed, down, start, size, at):
    out = jnp.dot(mixed[0], down[0, start : start + size, at], preferred_element_type=jnp.float32)
    for e in range(1, len(mixed)):
        out = out + jnp.dot(mixed[e], down[e, start : start + size, at], preferred_element_type=jnp.float32)
    return out


def down_first_kernel(width, first, kept, a, b, marks, total, scales):
    (down,) = kept
    experts, _, depth = down.shape
    rows = a.shape[0] // 2
    at = slice(2 * first, 2 * first + 128)
    square = a[:, at].astype(jnp.float32) + b[:, at].astype(jnp.float32)
    scale = lax.rsqrt((square[0:rows] + square[rows : 2 * rows]) / width + epsilon)
    scale = jnp.concatenate([scale, scale], axis=0)
    scales[...] = scale
    mixed = mix(a, b, scale[:, 0:1], marks, experts, first)
    piece = depth // GROUP
    for n in range(GROUP):
        at = slice(n * piece, (n + 1) * piece)
        total[:, at] = down_part(mixed, down, 0, first, at)


def down_first(a, b, marks, down, width, first):
    experts, _, depth = down.shape
    rows = a.shape[0] // 2
    size = experts * first * depth
    return with_weights(
        functools.partial(down_first_kernel, width, first),
        [a, b, marks],
        [down],
        [VMEM] * 3,
        [
            jax.ShapeDtypeStruct((rows, depth), jnp.float32),
            jax.ShapeDtypeStruct((2 * rows, 128), jnp.float32),
        ],
        [],
        "down_first",
        flops=2 * rows * size,
        bytes_accessed=2 * size,
    )


def down_last_kernel(whole, first, kept, a, b, scales, before, marks, *refs):
    (down,) = kept
    outs, total = refs[:-1], refs[-1]
    experts, hidden, depth = down.shape
    rows = total.shape[0]
    mixed = mix(a, b, scales[:, 0:1], marks, experts, hidden - first)
    piece = depth // GROUP
    for n in range(GROUP):
        at = slice(n * piece, (n + 1) * piece)
        total[:, at] = before[:, at] + down_part(mixed, down, first, hidden - first, at)
    mine, _, _ = where()
    for o in range(GROUP):
        if whole:
            matrix = rows_of(16, rows, lambda row: 8 * (row >> 1) + 2 * (mine ^ o) + (row & 1))
            outs[o][...] = pick(matrix, total[...])[0:8, :].astype(outs[o].dtype)
        else:
            at = pl.ds(pl.multiple_of((mine ^ o) * piece, 128), piece)
            outs[o][...] = total[:, at].astype(outs[o].dtype)


def down_last(a, b, scales, before, marks, down, first, whole):
    experts, hidden, depth = down.shape
    rows = a.shape[0] // 2
    size = experts * (hidden - first) * depth
    shape = (2 * GROUP, depth) if whole else (rows, depth // GROUP)
    shapes = [jax.ShapeDtypeStruct(shape, jnp.float32)]
    shapes += [jax.ShapeDtypeStruct(shape, jnp.bfloat16)] * (GROUP - 1)
    return with_weights(
        functools.partial(down_last_kernel, whole, first),
        [a, b, scales, before, marks],
        [down],
        [VMEM] * 5,
        shapes,
        [pltpu.VMEM((rows, depth), jnp.float32)],
        "down_last",
        flops=2 * rows * size,
        bytes_accessed=2 * size,
    )


def swap(value, axis, offset):
    size = lax.axis_size(axis)
    return lax.ppermute(value, axis, [(i, i ^ offset) for i in range(size)])


def body(tokens, norm_gain, routes, route_weights, w_gate, w_up, w_down):
    steps, rows, top = routes.shape
    experts, depth, hidden = w_gate.shape
    width = depth * lax.axis_size("narrow")
    first = hidden // 2
    note, gain, marks = prepare(norm_gain, routes, route_weights, experts)

    def around(value, scale):
        return [value] + [swap(value, "wide", scale * o) for o in range(1, GROUP)]

    head1, note = load_head(note, w_gate, w_up, 1)
    held, note = pack(note, around(tokens, GROUP))
    head0, _ = load_head(note, w_gate, w_up, 0)
    pieces = split(around(held, 1))
    for step in range(steps):
        a1, scaled = first_columns(pieces, gain, marks[step], head0, w_gate, w_up)
        b1 = swap(a1, "narrow", 1)
        a2 = last_columns(scaled, marks[step], head1, w_gate, w_up)
        b2 = swap(a2, "narrow", 1)
        final = step == steps - 1
        before, scales = down_first(a1, b1, marks[step], w_down, width, first)
        parts = down_last(a2, b2, scales, before, marks[step], w_down, first, final)
        own = add_up([parts[0]] + [swap(parts[o], "wide", o) for o in range(1, GROUP)])
        sums = around(own, GROUP)
        if final:
            return finish(sums, pieces)
        pieces = around(add_up([pieces[0]] + sums), 1)


def plain_body(tokens, norm_gain, routes, route_weights, w_gate, w_up, w_down):
    experts = w_gate.shape[0]
    steps, rows, top = routes.shape
    width = tokens.shape[1] * lax.axis_size("narrow")
    gain = norm_gain.astype(jnp.float32)
    named = (routes[..., None] == jnp.arange(experts, dtype=jnp.int32)).astype(jnp.float32)
    current = tokens
    for step in range(steps):
        values = current.astype(jnp.float32)
        squares = lax.psum(jnp.sum(values * values, axis=1), "narrow")
        normed = (values * lax.rsqrt(squares[:, None] / width + epsilon) * gain[None, :]).astype(jnp.bfloat16)
        normed = lax.all_gather(normed, "wide", axis=0, tiled=True)
        gate = jnp.einsum("rd,edf->erf", normed, w_gate, preferred_element_type=jnp.float32)
        up = jnp.einsum("rd,edf->erf", normed, w_up, preferred_element_type=jnp.float32)
        gate = lax.psum(gate.astype(jnp.bfloat16), "narrow").astype(jnp.float32)
        up = lax.psum(up.astype(jnp.bfloat16), "narrow").astype(jnp.float32)
        value = (jax.nn.silu(gate) * up).astype(jnp.bfloat16)
        out = jnp.einsum("erf,efd->erd", value, w_down, preferred_element_type=jnp.float32)
        share = jnp.sum(named[step] * route_weights[step][..., None], axis=1)
        combined = jnp.einsum("re,erd->rd", share, out, precision=lax.Precision.HIGHEST)
        summed = lax.psum_scatter(combined, "wide", scatter_dimension=0, tiled=True)
        current = (current.astype(jnp.float32) + summed).astype(jnp.bfloat16)
    return current


def solution(mesh):
    placed = (
        P("wide", "narrow"),
        P("narrow"),
        P(),
        P(),
        P(None, "narrow", "wide"),
        P(None, "narrow", "wide"),
        P(None, "wide", "narrow"),
    )

    def call(*args):
        tokens, _, routes, _, w_gate, _, _ = args
        wide, narrow = mesh.shape["wide"], mesh.shape["narrow"]
        depth, hidden = w_gate.shape[1] // narrow, w_gate.shape[2] // wide
        routes = args[2]
        fits = narrow == 2 and wide == GROUP * GROUP and routes.shape[2] == 2 and w_gate.shape[0] >= 2
        fits = fits and depth % (GROUP * 128) == 0 and hidden % 512 == 0 and routes.shape[1] == 2 * GROUP * GROUP
        return jax.shard_map(
            body if fits else plain_body, mesh=mesh, in_specs=placed, out_specs=P("wide", "narrow"), check_vma=False
        )(*args)

    return call
```

```python
import functools

import jax
import jax.numpy as jnp
from jax import lax
from jax.experimental import pallas as pl
from jax.experimental.pallas import tpu as pltpu
from jax.sharding import PartitionSpec as P

epsilon = 1e-05
MIB = 1 << 20
VMEM = pl.BlockSpec(memory_space=pltpu.VMEM)
HBM = pl.BlockSpec(memory_space=pltpu.HBM)
GROUP = 4
SLOTS = 4
KEPT = 2
NOTE = jax.ShapeDtypeStruct((8, 128), jnp.float32)
LIMIT = 2 * MIB
FIRST_LIMIT = 8 * MIB


def in_vmem(array):
    return pltpu.with_memory_space_constraint(array, pltpu.VMEM)


def in_hbm(array):
    return pltpu.with_memory_space_constraint(array, pltpu.HBM)


def with_weights(kernel, inputs, kept, specs, shapes, scratch, name, limit=None, **cost):
    count = len(inputs)

    def run(*refs):
        kernel(refs[count : count + len(kept)], *refs[:count], *refs[count + len(kept) :])

    more = {"cost_estimate": pl.CostEstimate(transcendentals=0, **cost)} if cost else {}
    return pl.pallas_call(
        run,
        in_specs=specs + [VMEM] * len(kept),
        out_specs=[VMEM] * len(shapes),
        out_shape=shapes,
        scratch_shapes=scratch,
        name=name,
        compiler_params=pltpu.CompilerParams(vmem_limit_bytes=limit or LIMIT),
        **more,
    )(*inputs, *[in_vmem(weight) for weight in kept])


def where():
    index = lax.axis_index("wide")
    return lax.rem(index, GROUP), lax.div(index, GROUP), index


def prepare_kernel(gain, named, weight, gain_out, note, *marks):
    note[...] = jnp.zeros_like(note)
    gain_out[...] = gain[...].astype(jnp.float32).reshape(gain_out.shape)
    steps, top, rows = named.shape
    same = lax.broadcasted_iota(jnp.int32, (rows, rows), 0) == lax.broadcasted_iota(jnp.int32, (rows, rows), 1)
    for step, mark in enumerate(marks):
        experts = mark.shape[1] // 2
        column = lax.broadcasted_iota(jnp.int32, (rows, 2 * experts), 1)
        expert = jnp.where(column < experts, column, column - experts)
        for k in range(top):
            chosen = jnp.sum(jnp.where(same, named[step, k : k + 1, :], 0), axis=1, keepdims=True)
            scale = jnp.sum(jnp.where(same, weight[step, k : k + 1, :], 0.0), axis=1, keepdims=True)
            value = jnp.where(column < experts, scale, 1.0)
            mark[k * rows : (k + 1) * rows, :] = jnp.where(chosen == expert, value, 0.0)


def prepare(gain, routes, route_weights, experts):
    steps, rows, top = routes.shape
    gain, note, *marks = pl.pallas_call(
        prepare_kernel,
        in_specs=[VMEM] * 3,
        out_specs=[VMEM] * (2 + steps),
        out_shape=[jax.ShapeDtypeStruct((1, gain.shape[0]), jnp.float32), NOTE]
        + [jax.ShapeDtypeStruct((top * rows, 2 * experts), jnp.float32)] * steps,
        name="prepare",
        compiler_params=pltpu.CompilerParams(vmem_limit_bytes=4 * MIB),
    )(in_hbm(gain), in_hbm(jnp.swapaxes(routes, 1, 2)), in_hbm(jnp.swapaxes(route_weights, 1, 2)))
    return note, gain, marks


def pack_kernel(note, a, b, c, d, out, note_out, rows):
    note_out[...] = note[...]
    for k, ref in enumerate((a, b, c, d)):
        rows[2 * k : 2 * k + 2, :] = ref[...].astype(jnp.float32)
    out[...] = rows[...].astype(out.dtype)


def pack(note, parts):
    depth = parts[0].shape[1]
    return pl.pallas_call(
        pack_kernel,
        in_specs=[VMEM] * 5,
        out_specs=[VMEM] * 2,
        out_shape=[jax.ShapeDtypeStruct((8, depth), jnp.bfloat16), NOTE],
        scratch_shapes=[pltpu.VMEM((8, depth), jnp.float32)],
        name="pack",
        compiler_params=pltpu.CompilerParams(vmem_limit_bytes=MIB),
    )(note, *parts)


def rows_of(count, all_rows, wanted):
    row = lax.broadcasted_iota(jnp.int32, (count, all_rows), 0)
    column = lax.broadcasted_iota(jnp.int32, (count, all_rows), 1)
    return jnp.where(wanted(row) == column, 1.0, 0.0).astype(jnp.bfloat16)


def pick(matrix, rows):
    return jnp.dot(matrix, rows.astype(jnp.bfloat16), preferred_element_type=jnp.float32)


def split_kernel(_, a, b, c, d, *refs):
    outs, rows = refs[:-1], refs[-1]
    mine, line, _ = where()
    for o, ref in enumerate((a, b, c, d)):
        rows[8 * o : 8 * o + 8, :] = ref[...].astype(jnp.float32)

    def source(row):
        return 8 * (((row >> 1) & 3) ^ mine) + 2 * ((row >> 3) ^ line) + (row & 1)

    count = rows.shape[0]
    rows[...] = pick(rows_of(count, count, source), rows[...])
    piece = outs[0].shape[1]
    for o in range(GROUP):
        at = pl.ds(pl.multiple_of((mine ^ o) * piece, 128), piece)
        outs[o][...] = rows[:, at].astype(jnp.bfloat16)


def split(parts):
    depth = parts[0].shape[1]
    rows = GROUP * parts[0].shape[0]
    return with_weights(
        split_kernel,
        parts,
        [],
        [VMEM] * 4,
        [jax.ShapeDtypeStruct((rows, depth // GROUP), jnp.bfloat16)] * GROUP,
        [pltpu.VMEM((rows, depth), jnp.float32)],
        "split",
    )


def sum_kernel(_, *refs):
    total = refs[0][...].astype(jnp.float32)
    for ref in refs[1:-1]:
        total = total + ref[...].astype(jnp.float32)
    refs[-1][...] = total.astype(refs[-1].dtype)


def add_up(parts):
    shapes = [jax.ShapeDtypeStruct(parts[0].shape, jnp.bfloat16)]
    return with_weights(sum_kernel, parts, [], [VMEM] * len(parts), shapes, [], "add_up")[0]


def finish_kernel(_, s0, s1, s2, s3, x0, x1, x2, x3, out, rows, total):
    mine, line, index = where()
    for k, ref in enumerate((s0, s1, s2, s3)):
        total[8 * k : 8 * k + 8, :] = ref[...].astype(jnp.float32)
    piece = x0.shape[1]
    for o, ref in enumerate((x0, x1, x2, x3)):
        at = pl.ds(pl.multiple_of((mine ^ o) * piece, 128), piece)
        rows[:, at] = ref[...].astype(jnp.float32)
    count = rows.shape[0]
    result = pick(rows_of(16, count, lambda row: 2 * index + row), rows[...])
    for k in range(GROUP):
        result = result + pick(rows_of(16, count, lambda row: 8 * k + 2 * line + row), total[...])
    out[...] = result[0:2, :].astype(out.dtype)


def finish(sums, pieces):
    depth = sums[0].shape[1]
    rows = pieces[0].shape[0]
    return with_weights(
        finish_kernel,
        [*sums, *pieces],
        [],
        [VMEM] * 8,
        [jax.ShapeDtypeStruct((2, depth), jnp.bfloat16)],
        [pltpu.VMEM((rows, depth), jnp.float32)] * 2,
        "finish",
    )[0]


def load_head_kernel(c, before, w_gate, w_up, head, note, sem):
    del before
    half = head.shape[2] // 2
    copies = []
    for e in range(head.shape[0]):
        for m, weight in enumerate((w_gate, w_up)):
            copies.append(
                pltpu.make_async_copy(
                    weight.at[e, :, pl.ds(c * half, half)],
                    head.at[e, :, pl.ds(m * half, half)],
                    sem.at[len(copies)],
                )
            )
    for copy in copies:
        copy.start()
    note[...] = jnp.zeros_like(note)
    for copy in copies:
        copy.wait()


def load_head(note, w_gate, w_up, c):
    _, depth, hidden = w_gate.shape
    return pl.pallas_call(
        functools.partial(load_head_kernel, c),
        in_specs=[VMEM] + [HBM] * 2,
        out_specs=[VMEM] * 2,
        out_shape=[pltpu.VMEM((KEPT, depth, hidden), w_gate.dtype), NOTE],
        scratch_shapes=[pltpu.SemaphoreType.DMA((2 * KEPT,))],
        name="load_head",
        cost_estimate=pl.CostEstimate(flops=0, bytes_accessed=12 * MIB, transcendentals=0),
        compiler_params=pltpu.CompilerParams(vmem_limit_bytes=LIMIT),
    )(note, in_hbm(w_gate), in_hbm(w_up))


def scale_up(pieces, gain, scaled, chosen, start):
    rows, piece = pieces[0].shape
    mine, _, _ = where()
    square = jnp.zeros((rows, 1), jnp.float32)
    for o, ref in enumerate(pieces):
        at = pl.ds(pl.multiple_of((mine ^ o) * piece, 128), piece)
        values = ref[...].astype(jnp.float32)
        square = square + jnp.sum(values * values, axis=1, keepdims=True)
        scaled[:, at] = (values * gain[:, at]).astype(jnp.bfloat16)
    coarse = square.astype(jnp.bfloat16)
    fine = (square - coarse.astype(jnp.float32)).astype(jnp.bfloat16)
    chosen[0:rows, start : start + 128] = jnp.broadcast_to(coarse, (rows, 128))
    chosen[rows : 2 * rows, start : start + 128] = jnp.broadcast_to(fine, (rows, 128))


def half_product(start, kept, scaled, marks, w_gate, w_up, chosen, ring, total, sem, before=None):
    (head,) = kept
    experts, depth, _ = w_gate.shape
    half = ring.shape[2] // 2
    rows = total.shape[1]
    block = ring.shape[1]
    streamed = [(e, q) for e in range(head.shape[0], experts) for q in range(depth // block)]
    resident = [(e, q) for e in range(head.shape[0]) for q in range(depth // block)]

    def copies(i):
        e, q = streamed[i]
        slot = i % SLOTS
        return [
            pltpu.make_async_copy(
                weight.at[e, pl.ds(q * block, block), pl.ds(start, half)],
                ring.at[slot, :, pl.ds(m * half, half)],
                sem.at[slot, m],
            )
            for m, weight in enumerate((w_gate, w_up))
        ]

    for i in range(min(SLOTS, len(streamed))):
        for copy in copies(i):
            copy.start()
    if before is not None:
        before()

    def add(e, q, weight):
        product = jnp.dot(
            scaled[:, q * block : (q + 1) * block], weight, preferred_element_type=jnp.float32
        )
        if q:
            total[e] += product
        else:
            total[e] = product

    ahead = max(len(resident) - len(streamed) // 2 + 1, 0)
    for i in range(ahead):
        e, q = resident[i]
        add(e, q, head[e, q * block : (q + 1) * block, :])
    left = resident[ahead:]
    for i in range(len(streamed)):
        for copy in copies(i):
            copy.wait()
        add(*streamed[i], ring[i % SLOTS])
        if i + SLOTS < len(streamed):
            for copy in copies(i + SLOTS):
                copy.start()
        if left and (i % 2 == 1 or i + 1 == len(streamed)):
            for e, q in left if i + 1 == len(streamed) else left[:1]:
                add(e, q, head[e, q * block : (q + 1) * block, :])
            left = left[1:]
    for k in range(2):
        picked = jnp.zeros((rows, 2 * half), jnp.float32)
        for e in range(experts):
            mark = marks[k * rows : (k + 1) * rows, experts + e : experts + e + 1]
            picked = jnp.where(mark > 0, total[e], picked)
        chosen[k * rows : (k + 1) * rows, 0 : 2 * half] = picked.astype(jnp.bfloat16)


def first_kernel(kept, x0, x1, x2, x3, gain, marks, w_gate, w_up, chosen, scaled, ring, total, sem):
    half_product(
        0, kept, scaled, marks, w_gate, w_up, chosen, ring, total, sem,
        before=lambda: scale_up((x0, x1, x2, x3), gain, scaled, chosen, ring.shape[2]),
    )


def last_kernel(kept, scaled, marks, w_gate, w_up, chosen, ring, total, sem):
    half_product(ring.shape[2] // 2, kept, scaled, marks, w_gate, w_up, chosen, ring, total, sem)


def half_columns(kernel, inputs, specs, kept, w_gate, w_up, outs, name):
    experts, depth, hidden = w_gate.shape
    rows = outs[0].shape[0] // 2
    count = experts * depth * hidden
    return with_weights(
        kernel,
        [*inputs, in_hbm(w_gate), in_hbm(w_up)],
        [kept],
        specs + [HBM] * 2,
        outs,
        [
            pltpu.VMEM((SLOTS, depth // GROUP, hidden), jnp.bfloat16),
            pltpu.VMEM((experts, rows, hidden), jnp.float32),
            pltpu.SemaphoreType.DMA((SLOTS, 2)),
        ],
        name,
        limit=FIRST_LIMIT,
        flops=2 * rows * count,
        bytes_accessed=2 * count,
    )


def first_columns(pieces, gain, marks, kept, w_gate, w_up):
    _, depth, hidden = w_gate.shape
    rows = pieces[0].shape[0]
    outs = [
        jax.ShapeDtypeStruct((2 * rows, hidden + 128), jnp.bfloat16),
        jax.ShapeDtypeStruct((rows, depth), jnp.bfloat16),
    ]
    return half_columns(
        first_kernel, [*pieces, gain, marks], [VMEM] * 6, kept, w_gate, w_up, outs, "gate_up_first"
    )


def last_columns(scaled, marks, kept, w_gate, w_up):
    outs = [jax.ShapeDtypeStruct((2 * scaled.shape[0], w_gate.shape[2]), jnp.bfloat16)]
    return half_columns(last_kernel, [scaled, marks], [VMEM] * 2, kept, w_gate, w_up, outs, "gate_up_last")[0]


def mix(a, b, scale, marks, experts, size):
    def both(start):
        return a[:, start : start + size].astype(jnp.float32) + b[:, start : start + size].astype(jnp.float32)

    rows = a.shape[0] // 2
    gate, up = both(0) * scale, both(size) * scale
    value = gate / (1.0 + jnp.exp(-gate)) * up
    return [
        (
            value[0:rows] * marks[0:rows, e : e + 1] + value[rows : 2 * rows] * marks[rows : 2 * rows, e : e + 1]
        ).astype(jnp.bfloat16)
        for e in range(experts)
    ]


def down_part(mixed, down, start, size, at):
    out = jnp.dot(mixed[0], down[0, start : start + size, at], preferred_element_type=jnp.float32)
    for e in range(1, len(mixed)):
        out = out + jnp.dot(mixed[e], down[e, start : start + size, at], preferred_element_type=jnp.float32)
    return out


def down_first_kernel(width, first, kept, a, b, marks, total, scales):
    (down,) = kept
    experts, _, depth = down.shape
    rows = a.shape[0] // 2
    at = slice(2 * first, 2 * first + 128)
    square = a[:, at].astype(jnp.float32) + b[:, at].astype(jnp.float32)
    scale = lax.rsqrt((square[0:rows] + square[rows : 2 * rows]) / width + epsilon)
    scale = jnp.concatenate([scale, scale], axis=0)
    scales[...] = scale
    mixed = mix(a, b, scale[:, 0:1], marks, experts, first)
    piece = depth // GROUP
    for n in range(GROUP):
        at = slice(n * piece, (n + 1) * piece)
        total[:, at] = down_part(mixed, down, 0, first, at)


def down_first(a, b, marks, down, width, first):
    experts, _, depth = down.shape
    rows = a.shape[0] // 2
    size = experts * first * depth
    return with_weights(
        functools.partial(down_first_kernel, width, first),
        [a, b, marks],
        [down],
        [VMEM] * 3,
        [
            jax.ShapeDtypeStruct((rows, depth), jnp.float32),
            jax.ShapeDtypeStruct((2 * rows, 128), jnp.float32),
        ],
        [],
        "down_first",
        flops=2 * rows * size,
        bytes_accessed=2 * size,
    )


def down_last_kernel(whole, first, kept, a, b, scales, before, marks, *refs):
    (down,) = kept
    outs, total = refs[:-1], refs[-1]
    experts, hidden, depth = down.shape
    rows = total.shape[0]
    mixed = mix(a, b, scales[:, 0:1], marks, experts, hidden - first)
    piece = depth // GROUP
    for n in range(GROUP):
        at = slice(n * piece, (n + 1) * piece)
        total[:, at] = before[:, at] + down_part(mixed, down, first, hidden - first, at)
    mine, _, _ = where()
    for o in range(GROUP):
        if whole:
            matrix = rows_of(16, rows, lambda row: 8 * (row >> 1) + 2 * (mine ^ o) + (row & 1))
            outs[o][...] = pick(matrix, total[...])[0:8, :].astype(outs[o].dtype)
        else:
            at = pl.ds(pl.multiple_of((mine ^ o) * piece, 128), piece)
            outs[o][...] = total[:, at].astype(outs[o].dtype)


def down_last(a, b, scales, before, marks, down, first, whole):
    experts, hidden, depth = down.shape
    rows = a.shape[0] // 2
    size = experts * (hidden - first) * depth
    shape = (2 * GROUP, depth) if whole else (rows, depth // GROUP)
    shapes = [jax.ShapeDtypeStruct(shape, jnp.float32)]
    shapes += [jax.ShapeDtypeStruct(shape, jnp.bfloat16)] * (GROUP - 1)
    return with_weights(
        functools.partial(down_last_kernel, whole, first),
        [a, b, scales, before, marks],
        [down],
        [VMEM] * 5,
        shapes,
        [pltpu.VMEM((rows, depth), jnp.float32)],
        "down_last",
        flops=2 * rows * size,
        bytes_accessed=2 * size,
    )


def down_piece_kernel(first, pieces, kept, a, b, scales, before, marks, *outs):
    (down,) = kept
    experts, hidden, depth = down.shape
    mixed = mix(a, b, scales[:, 0:1], marks, experts, hidden - first)
    piece = depth // GROUP
    mine, _, _ = where()
    for out, o in zip(outs, pieces):
        at = pl.ds(pl.multiple_of((mine ^ o) * piece, 128), piece)
        out[...] = (before[:, at] + down_part(mixed, down, first, hidden - first, at)).astype(out.dtype)


def down_pieces(a, b, scales, before, marks, down, first, pieces, kind):
    experts, hidden, depth = down.shape
    rows = a.shape[0] // 2
    size = experts * (hidden - first) * depth * len(pieces) // GROUP
    return with_weights(
        functools.partial(down_piece_kernel, first, pieces),
        [a, b, scales, before, marks],
        [down],
        [VMEM] * 5,
        [jax.ShapeDtypeStruct((rows, depth // GROUP), kind)] * len(pieces),
        [],
        "down_own" if pieces == (0,) else "down_sent",
        flops=2 * rows * size,
        bytes_accessed=2 * size,
    )


def swap(value, axis, offset):
    size = lax.axis_size(axis)
    return lax.ppermute(value, axis, [(i, i ^ offset) for i in range(size)])


def body(tokens, norm_gain, routes, route_weights, w_gate, w_up, w_down):
    steps, rows, top = routes.shape
    experts, depth, hidden = w_gate.shape
    width = depth * lax.axis_size("narrow")
    first = hidden // 2
    note, gain, marks = prepare(norm_gain, routes, route_weights, experts)

    def around(value, scale):
        return [value] + [swap(value, "wide", scale * o) for o in range(1, GROUP)]

    head1, note = load_head(note, w_gate, w_up, 1)
    held, note = pack(note, around(tokens, GROUP))
    head0, _ = load_head(note, w_gate, w_up, 0)
    pieces = split(around(held, 1))
    for step in range(steps):
        a1, scaled = first_columns(pieces, gain, marks[step], head0, w_gate, w_up)
        b1 = swap(a1, "narrow", 1)
        a2 = last_columns(scaled, marks[step], head1, w_gate, w_up)
        b2 = swap(a2, "narrow", 1)
        final = step == steps - 1
        before, scales = down_first(a1, b1, marks[step], w_down, width, first)
        if final:
            parts = down_last(a2, b2, scales, before, marks[step], w_down, first, True)
        else:
            given = (a2, b2, scales, before, marks[step], w_down, first)
            sent = down_pieces(*given, tuple(range(1, GROUP)), jnp.bfloat16)
            parts = [*down_pieces(*given, (0,), jnp.float32), *sent]
        own = add_up([parts[0]] + [swap(parts[o], "wide", o) for o in range(1, GROUP)])
        sums = around(own, GROUP)
        if final:
            return finish(sums, pieces)
        pieces = around(add_up([pieces[0]] + sums), 1)


def plain_body(tokens, norm_gain, routes, route_weights, w_gate, w_up, w_down):
    experts = w_gate.shape[0]
    steps, rows, top = routes.shape
    width = tokens.shape[1] * lax.axis_size("narrow")
    gain = norm_gain.astype(jnp.float32)
    named = (routes[..., None] == jnp.arange(experts, dtype=jnp.int32)).astype(jnp.float32)
    current = tokens
    for step in range(steps):
        values = current.astype(jnp.float32)
        squares = lax.psum(jnp.sum(values * values, axis=1), "narrow")
        normed = (values * lax.rsqrt(squares[:, None] / width + epsilon) * gain[None, :]).astype(jnp.bfloat16)
        normed = lax.all_gather(normed, "wide", axis=0, tiled=True)
        gate = jnp.einsum("rd,edf->erf", normed, w_gate, preferred_element_type=jnp.float32)
        up = jnp.einsum("rd,edf->erf", normed, w_up, preferred_element_type=jnp.float32)
        gate = lax.psum(gate.astype(jnp.bfloat16), "narrow").astype(jnp.float32)
        up = lax.psum(up.astype(jnp.bfloat16), "narrow").astype(jnp.float32)
        value = (jax.nn.silu(gate) * up).astype(jnp.bfloat16)
        out = jnp.einsum("erf,efd->erd", value, w_down, preferred_element_type=jnp.float32)
        share = jnp.sum(named[step] * route_weights[step][..., None], axis=1)
        combined = jnp.einsum("re,erd->rd", share, out, precision=lax.Precision.HIGHEST)
        summed = lax.psum_scatter(combined, "wide", scatter_dimension=0, tiled=True)
        current = (current.astype(jnp.float32) + summed).astype(jnp.bfloat16)
    return current


def solution(mesh):
    placed = (
        P("wide", "narrow"),
        P("narrow"),
        P(),
        P(),
        P(None, "narrow", "wide"),
        P(None, "narrow", "wide"),
        P(None, "wide", "narrow"),
    )

    def call(*args):
        tokens, _, routes, _, w_gate, _, _ = args
        wide, narrow = mesh.shape["wide"], mesh.shape["narrow"]
        depth, hidden = w_gate.shape[1] // narrow, w_gate.shape[2] // wide
        routes = args[2]
        fits = narrow == 2 and wide == GROUP * GROUP and routes.shape[2] == 2 and w_gate.shape[0] >= 2
        fits = fits and depth % (GROUP * 128) == 0 and hidden % 512 == 0 and routes.shape[1] == 2 * GROUP * GROUP
        return jax.shard_map(
            body if fits else plain_body, mesh=mesh, in_specs=placed, out_specs=P("wide", "narrow"), check_vma=False
        )(*args)

    return call
```
